256 devices in a mesh: ens: 16 (over x_lo, z), lat: 8 (over y, core), var: 2 (over x_hi).
Axes of the slice: x: 4 (x_hi: 2, x_lo: 2; x = x_hi * 2 + x_lo), y: 4, z: 8, core: 2. Of those that a mesh axis runs over, the one named last changes fastest.
Arguments:
- members: bfloat16 [16, 3, 12, 512, 1440], P('ens', None, 'var', 'lat'), may hold values from -6 to 6
- target: bfloat16 [3, 12, 512, 1440], P(None, 'var', 'lat'), may hold values from -6 to 6
- target_spectrum: bfloat16 [3, 12, 384, 2, 384], P(None, 'var', ('lat', 'ens')), may hold values from -5 to 5
- legendre: bfloat16 [384, 512, 384], P(('lat', 'ens')), may hold values from -0.25 to 0.25
- wavenum: int32 [384], replicated, may hold values from 0 to 383, each once
Outputs:
- member_grad: bfloat16 [16, 3, 12, 512, 1440], P('ens', None, 'var', 'lat')
- row_score: float32 [3, 12, 512], P(None, 'var', ('lat', 'ens'))
- spec_score: float32 [3, 12, 384], P(None, 'var', ('lat', 'ens'))
The draws below stay inside these ranges and needn't reach their ends.
Inputs may be any that keep to these rules, and one draw needn't show every extreme that they name: Slot s holds zonal wavenumber wavenum[s], each of 0 to 383 once; slots holding a value above 360 carry no coefficients.
All inputs are finite; a program needn't handle non-finite values.
Results may differ from the reference program's by a relative error of at most 0.006.
Values may be sent and summed in bfloat16 or wider, within the bound.
A program may use at most 128 MiB of HBM per device.

```python
import math
import jax
import jax.numpy as jnp
from jax import lax

NLON = 1440
NVAR = 12
LMAX = 360
LPAD = 384
MPAD = 384
BATCH = 3
MEMBERS = 16
NLAT = 512


def shard_levels(own_key, extent, split, smallest, high):
    factor_of, own = 1.0, jax.random.fold_in(own_key, 6)
    for position, blocks in split:
        heights = jnp.exp(jax.random.uniform(jax.random.fold_in(own, position), (blocks,), jnp.float32, smallest / len(split), high / len(split)))
        factor_of = factor_of * jnp.repeat(heights, extent[position] // blocks).reshape([-1 if axis == position else 1 for axis in range(len(extent))])
    return factor_of


def noise(rng, extent, scale, most, cuts=(), held_as=jnp.bfloat16):
    loudness = shard_levels(rng, extent, cuts, -0.22, 0.18) if cuts else 1.0
    entries = jax.random.normal(rng, extent, jnp.float32) * scale * loudness
    return jnp.minimum(jnp.maximum(entries, -most), most).astype(held_as)


def setup_inputs(seed: int = 0) -> dict:
    keys = jax.random.split(jax.random.key(seed), 6)
    return {
        "members": noise(keys[0], (MEMBERS, BATCH, NVAR, NLAT, NLON), 1.0, 6.0, ((0, 16), (2, 2), (3, 8))),
        "target": noise(keys[1], (BATCH, NVAR, NLAT, NLON), 1.0, 6.0, ((1, 2), (2, 8))),
        "target_spectrum": noise(keys[2], (BATCH, NVAR, MPAD, 2, LPAD), 0.7, 5.0, ((1, 2), (2, 128))),
        "legendre": noise(keys[3], (MPAD, NLAT, LPAD), NLAT ** -0.5, 0.25, ((0, 128),)),
        "wavenum": jax.random.permutation(keys[4], MPAD).astype(jnp.int32),
    }


smooth_width = 0.25

def soft_abs(difference):
    return jnp.sqrt(difference * difference + smooth_width * smooth_width)

def fourier_table(wave_part):
    points = jnp.arange(NLON, dtype=jnp.int32)
    phase_index = points[:, None] * wave_part[None, :].astype(jnp.int32) % NLON
    angles = phase_index.astype(jnp.float32) * (2.0 * math.pi / NLON)
    factor = 1.0 / math.sqrt(NLON)
    columns = jnp.stack([jnp.cos(angles) * factor, -jnp.sin(angles) * factor], axis=2)
    return columns.reshape(NLON, 2 * wave_part.shape[0]).astype(jnp.bfloat16)

def spectral_masks(wave_part):
    degree = jnp.arange(LPAD, dtype=jnp.int32)
    usable = (degree[None, :] >= wave_part[:, None]) & (degree[None, :] <= LMAX)
    double = jnp.where(wave_part == 0, 1.0, 2.0).astype(jnp.float32)
    weight = jnp.where(usable, double[:, None], jnp.zeros((), jnp.float32))
    return (usable, weight)

def crps_terms(ensemble, target_rows):
    members_count = ensemble.shape[0]
    offset = ensemble - target_rows[None]
    distance = soft_abs(offset)

    def accumulate(carry, other):
        spread, pair_slope = carry
        difference = ensemble - other[None]
        magnitude = soft_abs(difference)
        return ((spread + magnitude, pair_slope + difference / magnitude), None)
    start = (jnp.zeros_like(ensemble), jnp.zeros_like(ensemble))
    (spread, pair_slope), unused = lax.scan(accumulate, start, ensemble)
    ens_score = lax.optimization_barrier(jnp.mean(distance, axis=0)) - 0.5 * lax.optimization_barrier(jnp.mean(spread, axis=0)) / members_count
    return (ens_score, offset / distance - pair_slope / members_count)

def reference(members, target, target_spectrum, legendre, wavenum):
    columns = fourier_table(wavenum).astype(jnp.float32)
    usable, weight = spectral_masks(wavenum)
    legendre_wide = legendre.astype(jnp.float32)
    highest = lax.Precision.HIGHEST

    def forward(member):
        along_lon = jnp.dot(member.reshape(-1, NLON).astype(jnp.float32), columns, precision=highest, preferred_element_type=jnp.float32).astype(jnp.bfloat16)
        along_lon = along_lon.reshape(BATCH, NVAR, NLAT, MPAD, 2).astype(jnp.float32)
        spectra = jnp.einsum('stl,bvtsc->bvscl', legendre_wide, along_lon, precision=highest)
        return jnp.where(usable[:, None, :], spectra, 0.0).astype(jnp.bfloat16)
    spectra = lax.map(forward, members)

    def grid_item(paired):
        ens_score, point_slope = crps_terms(paired[0].astype(jnp.float32), paired[1].astype(jnp.float32))
        return (lax.optimization_barrier(jnp.mean(ens_score, axis=-1)), point_slope.astype(jnp.bfloat16))
    row_score, grid_slope = lax.map(grid_item, (jnp.moveaxis(members, 1, 0), target))

    def spectral_item(paired):
        ens_score, point_slope = crps_terms(paired[0].astype(jnp.float32), paired[1].astype(jnp.float32))
        scaled = weight[:, None, :]
        total = lax.optimization_barrier(jnp.sum(ens_score * scaled, axis=(2, 3))) / (2.0 * (LMAX + 1))
        return (total, (point_slope * scaled).astype(jnp.bfloat16))
    spec_score, spec_slope = lax.map(spectral_item, (jnp.moveaxis(spectra, 1, 0), target_spectrum))

    def adjoint(paired):
        slope_spec, slope_grid = paired
        along_back = jnp.einsum('stl,bvscl->bvtsc', legendre_wide, slope_spec.astype(jnp.float32), precision=highest).astype(jnp.bfloat16)
        spectral_part = jnp.dot(along_back.reshape(-1, 2 * MPAD).astype(jnp.float32), columns.T, precision=highest, preferred_element_type=jnp.float32)
        spectral_part = spectral_part.reshape(BATCH, NVAR, NLAT, NLON)
        return (slope_grid.astype(jnp.float32) + spectral_part).astype(jnp.bfloat16)
    member_grad = lax.map(adjoint, (jnp.moveaxis(spec_slope, 1, 0), jnp.moveaxis(grid_slope, 1, 0)))
    return (member_grad, row_score, spec_score)
```

```python
import functools
import math

import jax
import jax.numpy as jnp
from jax import lax
from jax.experimental import pallas as pl
from jax.experimental.pallas import tpu as pltpu
from jax.sharding import PartitionSpec as P

LMAX = 360
MESH = pl.DeviceIdType.MESH
F32 = jnp.float32
BF16 = jnp.bfloat16
WIDTH2 = 0.0625

ENS = 16
LATS = 8
FIELDS = 18
BAND = 64
ROWS = FIELDS * BAND
LON = 1440
SLOTS = 384
COLS = 2 * SLOTS
DEV_SLOTS = 3
PARTS = 2 * DEV_SLOTS
LATITUDES = 512
DEGREES = 384
PAIRS = FIELDS // 2
FULL = LON // 128
TAIL = LON - FULL * 128
BLOCKS = BAND // 16
FIELD_TILES = BLOCKS * FULL + 1
TILES = FIELDS * FIELD_TILES
OWN = -(-TILES // ENS)
CHUNKS = ((0, 17), (17, 17), (34, 17))
ENTRIES = FIELDS * PARTS
GROUPS = -(-ENTRIES // 8)


def crps_block(x, y):
    offset = x - y[None]
    square = offset * offset + WIDTH2
    inverse = lax.rsqrt(square)
    near = jnp.sum(square * inverse, axis=0)
    slope = jnp.zeros_like(x)
    spread = jnp.zeros_like(y)
    half = ENS // 2
    for shift in range(1, half):
        d = x - jnp.concatenate([x[shift:], x[:shift]], axis=0)
        s = d * d + WIDTH2
        r = lax.rsqrt(s)
        spread = spread + jnp.sum(s * r, axis=0)
        ratio = d * r
        back = jnp.concatenate([ratio[ENS - shift:], ratio[: ENS - shift]], axis=0)
        slope = slope + (ratio - back)
    d = x[:half] - x[half:]
    s = d * d + WIDTH2
    r = lax.rsqrt(s)
    spread = spread + jnp.sum(s * r, axis=0)
    ratio = d * r
    slope = slope + jnp.concatenate([ratio, -ratio], axis=0)
    pair_mean = (2.0 * spread + ENS * math.sqrt(WIDTH2)) * (0.5 / (ENS * ENS))
    return near * (1.0 / ENS) - pair_mean, offset * inverse - slope * (1.0 / ENS)


def body_kernel(
    mem, tgt, tsp, leg, waves, wnum,
    out, row_out, spec_out,
    tiles, own_target, got_a, got_d, table, send, got_b1, got_b2, got_c1, got_c2,
    wide, mixed, spectral, tspec, spec_sum, part, xs, ys, scores, score_sum, got_s,
    a_send, a_recv, d_send, d_recv, b1_send, b1_recv, b2_send, b2_recv,
    c1_send, c1_recv, c2_send, c2_recv, s_send, s_recv, own_sem,
):
    e = lax.axis_index("ens")
    q_me = lax.axis_index("lat")

    def ens_peer(k):
        return lax.rem(e + k, ENS)

    def lat_peer(k):
        return lax.rem(q_me + k, LATS)

    barrier = pltpu.get_barrier_semaphore()

    def greet_ens(k, carry):
        pl.semaphore_signal(barrier, inc=1, device_id={"ens": ens_peer(k)}, device_id_type=MESH)
        return carry

    def greet_lat(k, carry):
        pl.semaphore_signal(barrier, inc=1, device_id={"lat": lat_peer(k)}, device_id_type=MESH)
        return carry

    lax.fori_loop(1, ENS, greet_ens, 0)
    lax.fori_loop(1, LATS, greet_lat, 0)

    def retile(field, carry):
        rows = pl.multiple_of(field * BAND, BAND)
        for block in range(BLOCKS):
            for lane in range(FULL):
                tiles[field * FIELD_TILES + block * FULL + lane] = mem[
                    pl.ds(rows + 16 * block, 16), pl.ds(lane * 128, 128)
                ]
        tails = [
            mem[pl.ds(rows + 16 * block, 16), pl.ds(FULL * 128, TAIL)].astype(F32)
            for block in range(BLOCKS)
        ]
        tiles[field * FIELD_TILES + FIELD_TILES - 1] = jnp.concatenate(tails, axis=1).astype(BF16)
        return carry

    lax.fori_loop(0, FIELDS, retile, 0)
    tiles[pl.ds(TILES, ENS * OWN - TILES)] = jnp.zeros((ENS * OWN - TILES, 16, 128), BF16)

    def a_copy(chunk, peer, slot):
        first, count = CHUNKS[chunk]
        return pltpu.make_async_remote_copy(
            src_ref=tiles.at[pl.ds(peer * OWN + first, count)],
            dst_ref=got_a.at[slot, pl.ds(first, count)],
            send_sem=a_send.at[chunk, peer],
            recv_sem=a_recv.at[chunk, slot],
            device_id={"ens": peer},
            device_id_type=MESH,
        )

    def a_start(chunk):
        def step(k, carry):
            a_copy(chunk, ens_peer(k), e).start()
            return carry

        lax.fori_loop(1, ENS, step, 0)

    def a_wait(chunk):
        def step(k, carry):
            a_copy(chunk, e, ens_peer(k)).wait_recv()
            return carry

        lax.fori_loop(1, ENS, step, 0)

    pl.semaphore_wait(barrier, ENS - 1 + LATS - 1)
    a_start(0)
    own_copy = pltpu.make_async_copy(tiles.at[pl.ds(e * OWN, OWN)], got_a.at[e], own_sem)
    own_copy.start()

    def table_rows(index, carry):
        rows = pl.ds(pl.multiple_of(index * 64, 64), 64)
        wave = waves[rows, :].astype(F32)
        lane = lax.broadcasted_iota(jnp.int32, (64, 128), 1).astype(F32)
        row = lax.broadcasted_iota(jnp.int32, (64, 128), 0)

        def angles(turns):
            turns = turns - LON * jnp.floor(turns * (1.0 / LON))
            return turns * (2.0 * math.pi / LON)

        fine = angles(wave * lane)
        coarse = angles(wave * (128.0 * jnp.minimum(lane, 15.0)))
        cos_b, sin_b = jnp.cos(fine), jnp.sin(fine)
        factor = 1.0 / math.sqrt(LON)
        cos_a, sin_a = jnp.cos(coarse) * factor, jnp.sin(coarse) * factor
        real = lax.rem(row, 2) == 0
        first = jnp.where(real, cos_a, -sin_a)
        second = jnp.where(real, -sin_a, -cos_a)
        for lane_block in range(FULL + 1):
            width = min(128, LON - lane_block * 128)
            value = first[:, lane_block : lane_block + 1] * cos_b
            value = value + second[:, lane_block : lane_block + 1] * sin_b
            table[rows, pl.ds(lane_block * 128, width)] = value[:, :width].astype(BF16)
        return carry

    lax.fori_loop(0, COLS // 64, table_rows, 0)

    def forward(index, carry):
        lanes = pl.ds(pl.multiple_of(index * 384, 384), 384)
        value = lax.dot_general(
            table[...], mem[lanes, :], (((1,), (1,)), ((), ())), preferred_element_type=F32
        )
        send[:, lanes] = value.astype(BF16)
        return carry

    lax.fori_loop(0, ROWS // 384, forward, 0)

    per_lat = COLS // LATS
    per_ens = COLS // ENS

    def lat_copy(source, got, s_sem, r_sem, peer, slot):
        return pltpu.make_async_remote_copy(
            src_ref=source.at[pl.ds(peer * per_lat, per_lat)],
            dst_ref=got.at[pl.ds(slot * per_lat, per_lat)],
            send_sem=s_sem.at[peer],
            recv_sem=r_sem.at[slot],
            device_id={"lat": peer},
            device_id_type=MESH,
        )

    def ens_copy(source, got, s_sem, r_sem, peer, slot):
        return pltpu.make_async_remote_copy(
            src_ref=source.at[pl.ds(peer * per_ens, per_ens)],
            dst_ref=got.at[pl.ds(slot * per_ens, per_ens)],
            send_sem=s_sem.at[peer],
            recv_sem=r_sem.at[slot],
            device_id={"ens": peer},
            device_id_type=MESH,
        )

    def exchange(copy, count, peer_of, me, size, got, s_sem, r_sem):
        def start(k, carry):
            copy(send, got, s_sem, r_sem, peer_of(k), me).start()
            return carry

        lax.fori_loop(1, count, start, 0)
        mine = pl.ds(pl.multiple_of(me * size, size), size)
        got[mine, :] = send[mine, :]

    def finish(copy, count, peer_of, me, got, s_sem, r_sem):
        def wait(k, carry):
            copy(send, got, s_sem, r_sem, peer_of(k), me).wait_send()
            copy(send, got, s_sem, r_sem, me, peer_of(k)).wait_recv()
            return carry

        lax.fori_loop(1, count, wait, 0)

    def widen(got):
        def step(index, carry):
            rows = pl.ds(pl.multiple_of(index * 48, 48), 48)
            for pair in range(PAIRS):
                wide[pair, rows, :] = got[rows, pl.ds(pair * 128, 128)].astype(F32)
            return carry

        lax.fori_loop(0, COLS // 48, step, 0)

    exchange(lat_copy, LATS, lat_peer, q_me, per_lat, got_b1, b1_send, b1_recv)

    def target_tile(index, carry):
        tile = e * OWN + index
        field = tile // FIELD_TILES
        place = tile - field * FIELD_TILES

        @pl.when(jnp.logical_and(place < FIELD_TILES - 1, tile < TILES))
        def _():
            block = place // FULL
            lane = place - block * FULL
            rows = pl.multiple_of(field * BAND + block * 16, 16)
            own_target[index] = tgt[
                pl.ds(rows, 16), pl.ds(pl.multiple_of(lane * 128, 128), 128)
            ].astype(F32)

        @pl.when(jnp.logical_and(place == FIELD_TILES - 1, tile < TILES))
        def _():
            rows = pl.multiple_of(field * BAND, BAND)
            tails = [
                tgt[pl.ds(rows + 16 * block, 16), pl.ds(FULL * 128, TAIL)].astype(F32)
                for block in range(BLOCKS)
            ]
            own_target[index] = jnp.concatenate(tails, axis=1)

        @pl.when(tile >= TILES)
        def _():
            own_target[index] = jnp.zeros((16, 128), F32)

        return carry

    lax.fori_loop(0, OWN, target_tile, 0)
    field_first = (e * OWN) // FIELD_TILES
    scores[...] = jnp.zeros_like(scores)
    tspec[pl.ds(0, ENTRIES), :] = tsp[...].astype(F32)
    tspec[pl.ds(ENTRIES, GROUPS * 8 - ENTRIES), :] = jnp.zeros((GROUPS * 8 - ENTRIES, DEGREES), F32)
    spec_sum[...] = jnp.zeros_like(spec_sum)

    finish(lat_copy, LATS, lat_peer, q_me, got_b1, b1_send, b1_recv)
    widen(got_b1)

    def regroup_b(peer, carry):
        for pair in range(PAIRS):
            for twin in range(PARTS // 2):
                start = peer * PARTS + 2 * twin
                value = jnp.concatenate(
                    [
                        wide[pair, pl.ds(start, LATS, stride=per_lat), :],
                        wide[pair, pl.ds(start + 1, LATS, stride=per_lat), :],
                    ],
                    axis=0,
                )
                rows = pl.multiple_of(peer * per_ens + 16 * twin, 16)
                send[pl.ds(rows, 16), pl.ds(pair * 128, 128)] = value.astype(BF16)
        return carry

    lax.fori_loop(0, ENS, regroup_b, 0)
    exchange(ens_copy, ENS, ens_peer, e, per_ens, got_b2, b2_send, b2_recv)

    def grid_tile(index, carry):
        def load(member, inner):
            xs[member] = got_a[member, index].astype(F32)
            return inner

        lax.fori_loop(0, ENS, load, 0, unroll=True)
        for top in (0, 8):
            rows = pl.ds(top, 8)
            score, slope = crps_block(xs[:, rows, :], own_target[index, rows, :])
            ys[:, rows, :] = slope
            part[rows, :] = score

        def store(member, inner):
            got_a[member, index] = ys[member].astype(BF16)
            return inner

        lax.fori_loop(0, ENS, store, 0, unroll=True)
        tile = e * OWN + index
        field = tile // FIELD_TILES
        place = tile - field * FIELD_TILES
        local = field - field_first

        @pl.when(place < FIELD_TILES - 1)
        def _():
            rows = pl.ds(pl.multiple_of(place // FULL * 16, 16), 16)
            scores[local, rows, :] = scores[local, rows, :] + part[...]

        @pl.when(place == FIELD_TILES - 1)
        def _():
            segment = lax.broadcasted_iota(jnp.int32, (16, 128), 1) // TAIL
            for block in range(BLOCKS):
                rows = pl.ds(16 * block, 16)
                scores[local, rows, :] = scores[local, rows, :] + jnp.where(
                    segment == block, part[...], 0.0
                )

        return carry

    def d_copy(chunk, peer, slot):
        first, count = CHUNKS[chunk]
        return pltpu.make_async_remote_copy(
            src_ref=got_a.at[peer, pl.ds(first, count)],
            dst_ref=got_d.at[pl.ds(slot * OWN + first, count)],
            send_sem=d_send.at[chunk, peer],
            recv_sem=d_recv.at[chunk, slot],
            device_id={"ens": peer},
            device_id_type=MESH,
        )

    def d_start(chunk):
        def step(k, carry):
            d_copy(chunk, ens_peer(k), e).start()
            return carry

        lax.fori_loop(1, ENS, step, 0)

    def grid_chunk(chunk):
        a_wait(chunk)
        first, count = CHUNKS[chunk]
        lax.fori_loop(first, first + count, grid_tile, 0)

    own_copy.wait()
    grid_chunk(0)

    finish(ens_copy, ENS, ens_peer, e, got_b2, b2_send, b2_recv)
    a_start(1)
    a_start(2)
    widen(got_b2)
    low = lax.broadcasted_iota(jnp.int32, (16, 128), 1) < 64

    def swap(even, odd):
        first = jnp.where(low, even, pltpu.roll(odd, 64, 1))
        second = jnp.where(low, pltpu.roll(even, 64, 1), odd)
        return first, second

    half_rows = 2 * PAIRS * ENS

    def legendre_in(index, carry):
        pair = index // PARTS
        piece = index - pair * PARTS
        slot = piece // 2
        c = piece - 2 * slot
        row = pl.multiple_of((c * PAIRS + pair) * ENS, ENS)
        for twin in range(LATS // 2):
            start = piece * LATS + 2 * twin
            even = wide[pair, pl.ds(start, ENS, stride=per_ens), :]
            odd = wide[pair, pl.ds(start + 1, ENS, stride=per_ens), :]
            first, second = swap(even, odd)
            mixed[slot, pl.ds(row, ENS), pl.ds(twin * 128, 128)] = first.astype(BF16)
            mixed[slot, pl.ds(row + half_rows, ENS), pl.ds(twin * 128, 128)] = second.astype(BF16)
        return carry

    lax.fori_loop(0, PAIRS * PARTS, legendre_in, 0)
    for lane_block in range(DEGREES // 128):
        spectral[lane_block, pl.ds(ENTRIES * ENS, GROUPS * 8 * ENS - ENTRIES * ENS), :] = jnp.zeros(
            (GROUPS * 8 * ENS - ENTRIES * ENS, 128), F32
        )

    def analysis(slot, carry):
        value = jnp.dot(mixed[slot], leg[slot], preferred_element_type=F32)
        for field in range(FIELDS):
            for c in range(2):
                row = (field % 2) * half_rows + (c * PAIRS + field // 2) * ENS
                to = pl.multiple_of((field * PARTS + 2 * slot + c) * ENS, ENS)
                for lane_block in range(DEGREES // 128):
                    spectral[lane_block, pl.ds(to, ENS), :] = value[
                        row : row + ENS, lane_block * 128 : lane_block * 128 + 128
                    ]
        return carry

    lax.fori_loop(0, DEV_SLOTS, analysis, 0)

    first_slot = (q_me * ENS + e) * DEV_SLOTS
    slot_waves = [wnum[first_slot + s] for s in range(DEV_SLOTS)]

    def spectral_group(index, carry):
        group = index // (DEGREES // 128)
        lane_block = index - group * (DEGREES // 128)
        entry = group * 8 + lax.broadcasted_iota(jnp.int32, (8, 128), 0)
        slot = lax.rem(entry // 2, DEV_SLOTS)
        wave = jnp.where(slot == 0, slot_waves[0], jnp.where(slot == 1, slot_waves[1], slot_waves[2]))
        degree = lane_block * 128 + lax.broadcasted_iota(jnp.int32, (8, 128), 1)
        usable = jnp.logical_and(degree >= wave, degree <= LMAX)
        weight = jnp.where(usable, jnp.where(wave == 0, 1.0, 2.0), 0.0)
        base = group * (8 * ENS)
        x = jnp.stack(
            [spectral[lane_block, pl.ds(base + m, 8, stride=ENS), :] for m in range(ENS)], axis=0
        )
        x = jnp.where(usable[None], x, 0.0).astype(BF16).astype(F32)
        rows = pl.ds(pl.multiple_of(group * 8, 8), 8)
        y = tspec[rows, pl.ds(pl.multiple_of(lane_block * 128, 128), 128)]
        score, slope = crps_block(x, y)
        spec_sum[rows, :] = spec_sum[rows, :] + score * weight
        slope = slope * weight[None]
        for m in range(ENS):
            spectral[lane_block, pl.ds(base + m, 8, stride=ENS), :] = slope[m]
        return carry

    lax.fori_loop(0, GROUPS * (DEGREES // 128), spectral_group, 0)

    def synthesis(slot, carry):
        for field in range(FIELDS):
            for c in range(2):
                row = (field % 2) * half_rows + (c * PAIRS + field // 2) * ENS
                at = pl.multiple_of((field * PARTS + 2 * slot + c) * ENS, ENS)
                for lane_block in range(DEGREES // 128):
                    mixed[slot, pl.ds(row, ENS), pl.ds(lane_block * 128, 128)] = spectral[
                        lane_block, pl.ds(at, ENS), :
                    ].astype(BF16)
        value = lax.dot_general(
            mixed[slot, :, pl.ds(0, DEGREES)], leg[slot], (((1,), (1,)), ((), ())),
            preferred_element_type=F32,
        )
        for pair in range(PAIRS):
            for c in range(2):
                row = (c * PAIRS + pair) * ENS
                for twin in range(LATS // 2):
                    lanes = slice(twin * 128, twin * 128 + 128)
                    even, odd = swap(
                        value[row : row + ENS, lanes],
                        value[row + half_rows : row + half_rows + ENS, lanes],
                    )
                    start = (2 * slot + c) * LATS + 2 * twin
                    wide[pair, pl.ds(start, ENS, stride=per_ens), :] = even
                    wide[pair, pl.ds(start + 1, ENS, stride=per_ens), :] = odd
        return carry

    lax.fori_loop(0, DEV_SLOTS, synthesis, 0)

    def narrow(index, carry):
        rows = pl.ds(pl.multiple_of(index * 48, 48), 48)
        for pair in range(PAIRS):
            send[rows, pl.ds(pair * 128, 128)] = wide[pair, rows, :].astype(BF16)
        return carry

    lax.fori_loop(0, COLS // 48, narrow, 0)
    exchange(ens_copy, ENS, ens_peer, e, per_ens, got_c1, c1_send, c1_recv)
    d_start(0)

    for chunk in range(1, len(CHUNKS)):
        grid_chunk(chunk)
        d_start(chunk)
    own_back = pltpu.make_async_copy(got_a.at[e], got_d.at[pl.ds(e * OWN, OWN)], own_sem)
    own_back.start()

    lane = lax.broadcasted_iota(jnp.int32, (BAND, 128), 1)
    total = jnp.zeros((BAND, 128), F32)
    for local in range(3):
        rows_sum = jnp.sum(scores[local], axis=1, keepdims=True) * (1.0 / LON)
        total = total + jnp.where(lane == field_first + local, rows_sum, 0.0)
    score_sum[...] = total.reshape(LATS, 8, 128)

    def s_copy(peer, slot):
        return pltpu.make_async_remote_copy(
            src_ref=score_sum.at[peer // 2],
            dst_ref=got_s.at[slot],
            send_sem=s_send.at[peer],
            recv_sem=s_recv.at[slot],
            device_id={"ens": peer},
            device_id_type=MESH,
        )

    def s_start(k, carry):
        s_copy(ens_peer(k), e).start()
        return carry

    lax.fori_loop(1, ENS, s_start, 0)
    got_s[e] = score_sum[e // 2]

    finish(ens_copy, ENS, ens_peer, e, got_c1, c1_send, c1_recv)
    widen(got_c1)

    def regroup_c(band, carry):
        rows = pl.ds(pl.multiple_of(band * per_lat, per_lat), per_lat)
        for pair in range(PAIRS):
            send[rows, pl.ds(pair * 128, 128)] = wide[
                pair, pl.ds(band, per_lat, stride=LATS), :
            ].astype(BF16)
        return carry

    lax.fori_loop(0, LATS, regroup_c, 0)
    exchange(lat_copy, LATS, lat_peer, q_me, per_lat, got_c2, c2_send, c2_recv)
    spec_out[...] = jnp.sum(spec_sum[...], axis=1, keepdims=True) * (1.0 / (2.0 * (LMAX + 1)))
    finish(lat_copy, LATS, lat_peer, q_me, got_c2, c2_send, c2_recv)

    def d_wait(chunk):
        def step(k, carry):
            d_copy(chunk, ens_peer(k), e).wait_send()
            d_copy(chunk, e, ens_peer(k)).wait_recv()
            a_copy(chunk, ens_peer(k), e).wait_send()
            return carry

        lax.fori_loop(1, ENS, step, 0)

    def s_wait(k, carry):
        s_copy(ens_peer(k), e).wait_send()
        s_copy(e, ens_peer(k)).wait_recv()
        return carry

    for chunk in range(len(CHUNKS)):
        d_wait(chunk)
    lax.fori_loop(1, ENS, s_wait, 0)
    own_back.wait()
    row_out[...] = jnp.sum(got_s[...], axis=0)

    def backward(index, carry):
        lanes = pl.ds(pl.multiple_of(index * 128, 128), 128)
        value = lax.dot_general(
            got_c2[:, lanes], table[...], (((0,), (0,)), ((), ())), preferred_element_type=F32
        )
        for twin in range(2):
            field = 2 * index + twin
            rows = pl.multiple_of(field * BAND, BAND)
            tail = got_d[field * FIELD_TILES + FIELD_TILES - 1].astype(F32)
            for block in range(BLOCKS):
                at = twin * BAND + block * 16
                for lane_block in range(FULL):
                    both = value[at : at + 16, lane_block * 128 : lane_block * 128 + 128]
                    both = both + got_d[field * FIELD_TILES + block * FULL + lane_block].astype(F32)
                    out[pl.ds(rows + 16 * block, 16), pl.ds(lane_block * 128, 128)] = both.astype(BF16)
                moved = tail if block == 0 else pltpu.roll(tail, 128 - block * TAIL, 1)
                both = value[at : at + 16, FULL * 128 :] + moved[:, :TAIL]
                out[pl.ds(rows + 16 * block, 16), pl.ds(FULL * 128, TAIL)] = both.astype(BF16)
        return carry

    lax.fori_loop(0, PAIRS, backward, 0)


def body(members, target, target_spectrum, legendre, wavenum):
    ens_pos = lax.axis_index("ens")
    chunks = len(CHUNKS)
    vmem = pl.BlockSpec(memory_space=pltpu.VMEM)
    dma = pltpu.SemaphoreType.DMA
    member_grad, rows, spec = pl.pallas_call(
        body_kernel,
        out_shape=(
            jax.ShapeDtypeStruct((ROWS, LON), BF16),
            jax.ShapeDtypeStruct((8, 128), F32),
            jax.ShapeDtypeStruct((GROUPS * 8, 1), F32),
        ),
        in_specs=[vmem] * 5 + [pl.BlockSpec(memory_space=pltpu.SMEM)],
        out_specs=(vmem, vmem, vmem),
        scratch_shapes=[
            pltpu.VMEM((ENS * OWN, 16, 128), BF16),
            pltpu.VMEM((OWN, 16, 128), F32),
            pltpu.VMEM((ENS, OWN, 16, 128), BF16),
            pltpu.VMEM((ENS * OWN, 16, 128), BF16),
            pltpu.VMEM((COLS, LON), BF16),
            pltpu.VMEM((COLS, ROWS), BF16),
            pltpu.VMEM((COLS, ROWS), BF16),
            pltpu.VMEM((COLS, ROWS), BF16),
            pltpu.VMEM((COLS, ROWS), BF16),
            pltpu.VMEM((COLS, ROWS), BF16),
            pltpu.VMEM((PAIRS, COLS, 128), F32),
            pltpu.VMEM((DEV_SLOTS, FIELDS * 2 * ENS, LATITUDES), BF16),
            pltpu.VMEM((DEGREES // 128, GROUPS * 8 * ENS, 128), F32),
            pltpu.VMEM((GROUPS * 8, DEGREES), F32),
            pltpu.VMEM((GROUPS * 8, 128), F32),
            pltpu.VMEM((16, 128), F32),
            pltpu.VMEM((ENS, 16, 128), F32),
            pltpu.VMEM((ENS, 16, 128), F32),
            pltpu.VMEM((3, BAND, 128), F32),
            pltpu.VMEM((LATS, 8, 128), F32),
            pltpu.VMEM((ENS, 8, 128), F32),
            dma((chunks, ENS)), dma((chunks, ENS)),
            dma((chunks, ENS)), dma((chunks, ENS)),
            dma((LATS,)), dma((LATS,)),
            dma((ENS,)), dma((ENS,)),
            dma((ENS,)), dma((ENS,)),
            dma((LATS,)), dma((LATS,)),
            dma((ENS,)), dma((ENS,)),
            dma,
        ],
        compiler_params=pltpu.CompilerParams(
            collective_id=0, has_side_effects=True, vmem_limit_bytes=60 * 2**20
        ),
    )(
        members.reshape(ROWS, LON),
        target.reshape(ROWS, LON),
        target_spectrum.reshape(ENTRIES, DEGREES),
        legendre,
        jnp.repeat(wavenum, 2).reshape(COLS, 1),
        wavenum,
    )
    batches, fields = members.shape[1], members.shape[2]
    member_grad = member_grad.reshape(members.shape)
    own = lax.dynamic_slice_in_dim(rows, lax.rem(ens_pos, 2) * 4, 4, 0)[:, :FIELDS]
    row_score = own.T.reshape(batches, fields, 4)
    spec = spec.reshape(-1)[:ENTRIES].reshape(FIELDS, DEV_SLOTS, 2)
    spec_score = (spec[..., 0] + spec[..., 1]).reshape(batches, fields, DEV_SLOTS)
    return (member_grad, row_score, spec_score)


def solution(mesh):
    in_specs = (
        P("ens", None, "var", "lat", None),
        P(None, "var", "lat", None),
        P(None, "var", ("lat", "ens"), None, None),
        P(("lat", "ens"), None, None),
        P(),
    )
    out_specs = (
        P("ens", None, "var", "lat", None),
        P(None, "var", ("lat", "ens")),
        P(None, "var", ("lat", "ens")),
    )
    return jax.shard_map(body, mesh=mesh, in_specs=in_specs, out_specs=out_specs, check_vma=False)
```

```python
import functools
import math

import jax
import jax.numpy as jnp
from jax import lax
from jax.experimental import pallas as pl
from jax.experimental.pallas import tpu as pltpu
from jax.sharding import PartitionSpec as P

LMAX = 360
MESH = pl.DeviceIdType.MESH
F32 = jnp.float32
BF16 = jnp.bfloat16
WIDTH2 = 0.0625

ENS = 16
ZS = 8
XS = 2
LATS = 8
PLANE = LATS * XS
FIELDS = 18
BATCHES = 3
BAND = 64
ROWS = FIELDS * BAND
LON = 1440
SLOTS = 384
COLS = 2 * SLOTS
DEV_SLOTS = 3
PARTS = 2 * DEV_SLOTS
LATITUDES = 512
DEGREES = 384
PAIRS = FIELDS // 2
FULL = LON // 128
TAIL = LON - FULL * 128
BLOCKS = BAND // 16
FIELD_TILES = BLOCKS * FULL + 1
TILES = FIELDS * FIELD_TILES
OWN = -(-TILES // ENS)
CHUNKS = ((0, 9), (9, 18), (27, 24))
LOADS = 3
STEPS = 6
ENTRIES = FIELDS * PARTS
GROUPS = -(-ENTRIES // 8)


def crps_block(x, y):
    offset = x - y[None]
    square = offset * offset + WIDTH2
    inverse = lax.rsqrt(square)
    near = jnp.sum(square * inverse, axis=0)
    slope = jnp.zeros_like(x)
    spread = jnp.zeros_like(y)
    half = ENS // 2
    for shift in range(1, half):
        d = x - jnp.concatenate([x[shift:], x[:shift]], axis=0)
        s = d * d + WIDTH2
        r = lax.rsqrt(s)
        spread = spread + jnp.sum(s * r, axis=0)
        ratio = d * r
        back = jnp.concatenate([ratio[ENS - shift:], ratio[: ENS - shift]], axis=0)
        slope = slope + (ratio - back)
    d = x[:half] - x[half:]
    s = d * d + WIDTH2
    r = lax.rsqrt(s)
    spread = spread + jnp.sum(s * r, axis=0)
    ratio = d * r
    slope = slope + jnp.concatenate([ratio, -ratio], axis=0)
    pair_mean = (2.0 * spread + ENS * math.sqrt(WIDTH2)) * (0.5 / (ENS * ENS))
    return near * (1.0 / ENS) - pair_mean, offset * inverse - slope * (1.0 / ENS)


def body_kernel(
    mem_hbm, tgt_hbm, tsp, leg_hbm, wave_rows, wnum,
    got_d, grad_hbm, small,
    mem, tgt, leg, tiles, own_target, got_a, stage_a, stage_d, grad, table, send, got_b1, got_b2, got_c1, got_c2,
    wide, mixed, spectral, tspec, spec_sum, part, xs, ys, scores, score_sum, got_s,
    ax_send, ax_recv, dx_send, dx_recv, a_send, a_recv, d_send, d_recv, b1_send, b1_recv, b2_send, b2_recv,
    c1_send, c1_recv, c2_send, c2_recv, s_send, s_recv, mem_sem, tgt_sem, leg_sem, grad_sem, keep_sem,
):
    e = lax.axis_index("ens")
    q_me = lax.axis_index("lat")

    def ens_peer(k):
        return lax.rem(e + k, ENS)

    x_me = e // ZS
    z_me = e - x_me * ZS
    partner = (1 - x_me) * ZS + z_me
    g_me = q_me * XS + x_me

    def z_peer(k):
        return lax.rem(z_me + k, ZS)

    def plane_peer(k):
        return lax.rem(g_me + k, PLANE)

    def mem_load(index):
        rows = pl.ds(index * (ROWS // LOADS), ROWS // LOADS)
        return pltpu.make_async_copy(mem_hbm.at[rows], mem.at[rows], mem_sem.at[index])

    tgt_load = pltpu.make_async_copy(tgt_hbm, tgt, tgt_sem)
    leg_load = pltpu.make_async_copy(leg_hbm, leg, leg_sem)
    for index in range(LOADS):
        mem_load(index).start()
    tgt_load.start()
    leg_load.start()
    barrier = pltpu.get_barrier_semaphore()

    def greet_ens(k, carry):
        pl.semaphore_signal(barrier, inc=1, device_id={"ens": ens_peer(k)}, device_id_type=MESH)
        return carry

    def greet_plane(k, carry):
        for x in range(XS):
            pl.semaphore_signal(
                barrier,
                inc=1,
                device_id={"ens": x * ZS + z_me, "lat": lax.rem(q_me + k, LATS)},
                device_id_type=MESH,
            )
        return carry

    lax.fori_loop(1, ENS, greet_ens, 0)
    lax.fori_loop(1, LATS, greet_plane, 0)

    def retile(field, carry):
        rows = pl.multiple_of(field * BAND, BAND)
        for block in range(BLOCKS):
            for lane in range(FULL):
                tiles[field * FIELD_TILES + block * FULL + lane] = mem[
                    pl.ds(rows + 16 * block, 16), pl.ds(lane * 128, 128)
                ]
        tails = [
            mem[pl.ds(rows + 16 * block, 16), pl.ds(FULL * 128, TAIL)].astype(F32)
            for block in range(BLOCKS)
        ]
        tiles[field * FIELD_TILES + FIELD_TILES - 1] = jnp.concatenate(tails, axis=1).astype(BF16)
        return carry

    for index in range(LOADS):
        mem_load(index).wait()
        lax.fori_loop(index * (FIELDS // LOADS), (index + 1) * (FIELDS // LOADS), retile, 0)
    tiles[pl.ds(TILES, ENS * OWN - TILES)] = jnp.zeros((ENS * OWN - TILES, 16, 128), BF16)

    def ax_copy(chunk, z):
        first, count = CHUNKS[chunk]
        return pltpu.make_async_remote_copy(
            src_ref=tiles.at[pl.ds(((1 - x_me) * ZS + z) * OWN + first, count)],
            dst_ref=stage_a.at[z, pl.ds(first, count)],
            send_sem=ax_send.at[chunk, z],
            recv_sem=ax_recv.at[chunk, z],
            device_id={"ens": partner},
            device_id_type=MESH,
        )

    def a_copy(chunk, z, slot):
        first, count = CHUNKS[chunk]
        return pltpu.make_async_remote_copy(
            src_ref=tiles.at[pl.ds((x_me * ZS + z) * OWN + first, count)],
            dst_ref=got_a.at[slot, pl.ds(first, count)],
            send_sem=a_send.at[chunk, z],
            recv_sem=a_recv.at[chunk, slot],
            device_id={"ens": x_me * ZS + z},
            device_id_type=MESH,
        )

    def a_pass(chunk, z, slot):
        first, count = CHUNKS[chunk]
        return pltpu.make_async_remote_copy(
            src_ref=stage_a.at[z, pl.ds(first, count)],
            dst_ref=got_a.at[slot, pl.ds(first, count)],
            send_sem=a_send.at[chunk, ZS + z],
            recv_sem=a_recv.at[chunk, slot],
            device_id={"ens": x_me * ZS + z},
            device_id_type=MESH,
        )

    def ax_start(chunk):
        def step(k, carry):
            ax_copy(chunk, z_peer(k)).start()
            return carry

        lax.fori_loop(1, ZS + 1, step, 0)

    def a_start(chunk):
        def step(k, carry):
            a_copy(chunk, z_peer(k), e).start()
            return carry

        lax.fori_loop(1, ZS, step, 0)
        first, count = CHUNKS[chunk]
        got_a[e, pl.ds(first, count)] = tiles[pl.ds(e * OWN + first, count)]

    def a_forward(chunk):
        def step(k, carry):
            ax_copy(chunk, z_peer(k)).wait_recv()
            a_pass(chunk, z_peer(k), partner).start()
            return carry

        lax.fori_loop(1, ZS, step, 0)
        ax_copy(chunk, z_me).wait_recv()
        first, count = CHUNKS[chunk]
        got_a[partner, pl.ds(first, count)] = stage_a[z_me, pl.ds(first, count)]

    def a_wait(chunk):
        def step(k, carry):
            a_copy(chunk, z_me, x_me * ZS + z_peer(k)).wait_recv()
            a_pass(chunk, z_me, (1 - x_me) * ZS + z_peer(k)).wait_recv()
            return carry

        lax.fori_loop(1, ZS, step, 0)

    def a_done(chunk):
        def step(k, carry):
            a_copy(chunk, z_peer(k), e).wait_send()
            a_pass(chunk, z_peer(k), partner).wait_send()
            return carry

        def step_x(z, carry):
            ax_copy(chunk, z).wait_send()
            return carry

        lax.fori_loop(1, ZS, step, 0)
        lax.fori_loop(0, ZS, step_x, 0)

    pl.semaphore_wait(barrier, ENS - 1 + XS * (LATS - 1))
    for chunk in range(len(CHUNKS)):
        a_start(chunk)
        if chunk == 0:
            ax_start(0)

    def table_rows(index, carry):
        rows = pl.ds(pl.multiple_of(index * 64, 64), 64)
        lane = lax.broadcasted_iota(jnp.int32, (64, 128), 1).astype(F32)
        row = lax.broadcasted_iota(jnp.int32, (64, 128), 0)
        group = wave_rows[pl.ds(index // 4, 1), :].astype(F32)
        at = lax.rem(index, 4) * 32 + row // 2
        wave = jnp.sum(
            jnp.where(lax.broadcasted_iota(jnp.int32, (64, 128), 1) == at, group, 0.0),
            axis=1,
            keepdims=True,
        )

        def angles(turns):
            turns = turns - LON * jnp.floor(turns * (1.0 / LON))
            return turns * (2.0 * math.pi / LON)

        fine = angles(wave * lane)
        coarse = angles(wave * (128.0 * jnp.minimum(lane, 15.0)))
        cos_b, sin_b = jnp.cos(fine), jnp.sin(fine)
        factor = 1.0 / math.sqrt(LON)
        cos_a, sin_a = jnp.cos(coarse) * factor, jnp.sin(coarse) * factor
        real = lax.rem(row, 2) == 0
        first = jnp.where(real, cos_a, -sin_a)
        second = jnp.where(real, -sin_a, -cos_a)
        for lane_block in range(FULL + 1):
            width = min(128, LON - lane_block * 128)
            value = first[:, lane_block : lane_block + 1] * cos_b
            value = value + second[:, lane_block : lane_block + 1] * sin_b
            table[rows, pl.ds(lane_block * 128, width)] = value[:, :width].astype(BF16)
        return carry

    lax.fori_loop(0, COLS // 64, table_rows, 0)

    def forward(index, carry):
        lanes = pl.ds(pl.multiple_of(index * 384, 384), 384)
        value = lax.dot_general(
            table[...], mem[lanes, :], (((1,), (1,)), ((), ())), preferred_element_type=F32
        )
        send[:, lanes] = value.astype(BF16)
        return carry

    lax.fori_loop(0, ROWS // 384, forward, 0)

    per_plane = COLS // PLANE
    per_z = COLS // ZS

    def plane_copy(source, got, s_sem, r_sem, peer, slot):
        return pltpu.make_async_remote_copy(
            src_ref=source.at[pl.ds(peer * per_plane, per_plane)],
            dst_ref=got.at[pl.ds(slot * per_plane, per_plane)],
            send_sem=s_sem.at[peer],
            recv_sem=r_sem.at[slot],
            device_id={"ens": lax.rem(peer, XS) * ZS + z_me, "lat": peer // XS},
            device_id_type=MESH,
        )

    def z_copy(source, got, s_sem, r_sem, peer, slot):
        return pltpu.make_async_remote_copy(
            src_ref=source.at[pl.ds(peer * per_z, per_z)],
            dst_ref=got.at[pl.ds(slot * per_z, per_z)],
            send_sem=s_sem.at[peer],
            recv_sem=r_sem.at[slot],
            device_id={"ens": x_me * ZS + peer},
            device_id_type=MESH,
        )

    def exchange(copy, count, peer_of, me, size, got, s_sem, r_sem):
        def start(k, carry):
            copy(send, got, s_sem, r_sem, peer_of(k), me).start()
            return carry

        lax.fori_loop(1, count, start, 0)
        mine = pl.ds(pl.multiple_of(me * size, size), size)
        got[mine, :] = send[mine, :]

    def finish(copy, count, peer_of, me, got, s_sem, r_sem):
        def wait(k, carry):
            copy(send, got, s_sem, r_sem, peer_of(k), me).wait_send()
            copy(send, got, s_sem, r_sem, me, peer_of(k)).wait_recv()
            return carry

        lax.fori_loop(1, count, wait, 0)

    def widen(got):
        def step(index, carry):
            rows = pl.ds(pl.multiple_of(index * 48, 48), 48)
            for pair in range(PAIRS):
                wide[pair, rows, :] = got[rows, pl.ds(pair * 128, 128)].astype(F32)
            return carry

        lax.fori_loop(0, COLS // 48, step, 0)

    exchange(plane_copy, PLANE, plane_peer, g_me, per_plane, got_b1, b1_send, b1_recv)

    tgt_load.wait()

    def target_tile(index, carry):
        tile = e * OWN + index
        field = tile // FIELD_TILES
        place = tile - field * FIELD_TILES

        @pl.when(jnp.logical_and(place < FIELD_TILES - 1, tile < TILES))
        def _():
            block = place // FULL
            lane = place - block * FULL
            rows = pl.multiple_of(field * BAND + block * 16, 16)
            own_target[index] = tgt[
                pl.ds(rows, 16), pl.ds(pl.multiple_of(lane * 128, 128), 128)
            ].astype(F32)

        @pl.when(jnp.logical_and(place == FIELD_TILES - 1, tile < TILES))
        def _():
            rows = pl.multiple_of(field * BAND, BAND)
            tails = [
                tgt[pl.ds(rows + 16 * block, 16), pl.ds(FULL * 128, TAIL)].astype(F32)
                for block in range(BLOCKS)
            ]
            own_target[index] = jnp.concatenate(tails, axis=1)

        @pl.when(tile >= TILES)
        def _():
            own_target[index] = jnp.zeros((16, 128), F32)

        return carry

    lax.fori_loop(0, OWN, target_tile, 0)
    field_first = (e * OWN) // FIELD_TILES
    scores[...] = jnp.zeros_like(scores)
    for b in range(BATCHES):
        for v in range(FIELDS // BATCHES):
            for s in range(DEV_SLOTS):
                row = (b * (FIELDS // BATCHES) + v) * PARTS + 2 * s
                tspec[pl.ds(row, 2), :] = tsp[b, v, s].astype(F32)
    tspec[pl.ds(ENTRIES, GROUPS * 8 - ENTRIES), :] = jnp.zeros((GROUPS * 8 - ENTRIES, DEGREES), F32)
    spec_sum[...] = jnp.zeros_like(spec_sum)

    a_forward(0)
    finish(plane_copy, PLANE, plane_peer, g_me, got_b1, b1_send, b1_recv)
    widen(got_b1)

    def regroup_b(peer, carry):
        for pair in range(PAIRS):
            for piece in range(PARTS):
                value = wide[pair, pl.ds(peer * PARTS + piece, PLANE, stride=per_plane), :]
                rows = pl.multiple_of(peer * per_z + PLANE * piece, PLANE)
                send[pl.ds(rows, PLANE), pl.ds(pair * 128, 128)] = value.astype(BF16)
        return carry

    lax.fori_loop(0, ZS, regroup_b, 0)
    exchange(z_copy, ZS, z_peer, z_me, per_z, got_b2, b2_send, b2_recv)
    ax_start(1)
    ax_start(2)

    def grid_tile(index, carry):
        def load(member, inner):
            xs[member] = got_a[member, index].astype(F32)
            return inner

        lax.fori_loop(0, ENS, load, 0, unroll=True)
        for top in (0, 8):
            rows = pl.ds(top, 8)
            score, slope = crps_block(xs[:, rows, :], own_target[index, rows, :])
            ys[:, rows, :] = slope
            part[rows, :] = score

        def store(member, inner):
            got_a[member, index] = ys[member].astype(BF16)
            return inner

        lax.fori_loop(0, ENS, store, 0, unroll=True)
        tile = e * OWN + index
        field = tile // FIELD_TILES
        place = tile - field * FIELD_TILES
        local = field - field_first

        @pl.when(place < FIELD_TILES - 1)
        def _():
            rows = pl.ds(pl.multiple_of(place // FULL * 16, 16), 16)
            scores[local, rows, :] = scores[local, rows, :] + part[...]

        @pl.when(place == FIELD_TILES - 1)
        def _():
            segment = lax.broadcasted_iota(jnp.int32, (16, 128), 1) // TAIL
            for block in range(BLOCKS):
                rows = pl.ds(16 * block, 16)
                scores[local, rows, :] = scores[local, rows, :] + jnp.where(
                    segment == block, part[...], 0.0
                )

        return carry

    def dx_copy(chunk, z):
        first, count = CHUNKS[chunk]
        return pltpu.make_async_remote_copy(
            src_ref=got_a.at[(1 - x_me) * ZS + z, pl.ds(first, count)],
            dst_ref=stage_d.at[z, pl.ds(first, count)],
            send_sem=dx_send.at[chunk, z],
            recv_sem=dx_recv.at[chunk, z],
            device_id={"ens": partner},
            device_id_type=MESH,
        )

    def d_copy(chunk, z, slot):
        first, count = CHUNKS[chunk]
        return pltpu.make_async_remote_copy(
            src_ref=got_a.at[x_me * ZS + z, pl.ds(first, count)],
            dst_ref=got_d.at[pl.ds(slot * OWN + first, count)],
            send_sem=d_send.at[chunk, z],
            recv_sem=d_recv.at[chunk, slot],
            device_id={"ens": x_me * ZS + z},
            device_id_type=MESH,
        )

    def d_pass(chunk, z, slot):
        first, count = CHUNKS[chunk]
        return pltpu.make_async_remote_copy(
            src_ref=stage_d.at[z, pl.ds(first, count)],
            dst_ref=got_d.at[pl.ds(slot * OWN + first, count)],
            send_sem=d_send.at[chunk, ZS + z],
            recv_sem=d_recv.at[chunk, slot],
            device_id={"ens": x_me * ZS + z},
            device_id_type=MESH,
        )

    def d_keep(chunk):
        first, count = CHUNKS[chunk]
        return pltpu.make_async_copy(
            got_a.at[e, pl.ds(first, count)],
            got_d.at[pl.ds(e * OWN + first, count)],
            keep_sem.at[chunk, 0],
        )

    def d_cross(chunk):
        first, count = CHUNKS[chunk]
        return pltpu.make_async_copy(
            stage_d.at[z_me, pl.ds(first, count)],
            got_d.at[pl.ds(partner * OWN + first, count)],
            keep_sem.at[chunk, 1],
        )

    def dx_start(chunk):
        def step(k, carry):
            dx_copy(chunk, z_peer(k)).start()
            return carry

        lax.fori_loop(1, ZS + 1, step, 0)

    def d_start(chunk):
        def step(k, carry):
            d_copy(chunk, z_peer(k), e).start()
            return carry

        lax.fori_loop(1, ZS, step, 0)
        d_keep(chunk).start()

    def d_forward(chunk):
        def step(k, carry):
            dx_copy(chunk, z_peer(k)).wait_recv()
            d_pass(chunk, z_peer(k), partner).start()
            return carry

        lax.fori_loop(1, ZS, step, 0)
        dx_copy(chunk, z_me).wait_recv()
        d_cross(chunk).start()

    def d_wait(chunk):
        def step(k, carry):
            d_copy(chunk, z_peer(k), e).wait_send()
            d_pass(chunk, z_peer(k), partner).wait_send()
            d_copy(chunk, z_me, x_me * ZS + z_peer(k)).wait_recv()
            d_pass(chunk, z_me, (1 - x_me) * ZS + z_peer(k)).wait_recv()
            return carry

        def step_x(z, carry):
            dx_copy(chunk, z).wait_send()
            return carry

        lax.fori_loop(1, ZS, step, 0)
        lax.fori_loop(0, ZS, step_x, 0)
        d_keep(chunk).wait()
        d_cross(chunk).wait()

    def grid_chunk(chunk):
        a_wait(chunk)
        first, count = CHUNKS[chunk]
        lax.fori_loop(first, first + count, grid_tile, 0)

    grid_chunk(0)
    dx_start(0)

    a_forward(1)
    finish(z_copy, ZS, z_peer, z_me, got_b2, b2_send, b2_recv)
    a_forward(2)
    widen(got_b2)
    low = lax.broadcasted_iota(jnp.int32, (16, 128), 1) < 64

    def swap(even, odd):
        first = jnp.where(low, even, pltpu.roll(odd, 64, 1))
        second = jnp.where(low, pltpu.roll(even, 64, 1), odd)
        return first, second

    half_rows = 2 * PAIRS * ENS

    def legendre_in(index, carry):
        pair = index // PARTS
        piece = index - pair * PARTS
        slot = piece // 2
        c = piece - 2 * slot
        row = pl.multiple_of((c * PAIRS + pair) * ENS, ENS)
        for twin in range(LATS // 2):
            start = piece * PLANE + 2 * XS * twin
            rows = [wide[pair, pl.ds(start + i, ZS, stride=per_z), :] for i in range(2 * XS)]
            even = jnp.concatenate(rows[:XS], axis=0)
            odd = jnp.concatenate(rows[XS:], axis=0)
            first, second = swap(even, odd)
            mixed[slot, pl.ds(row, ENS), pl.ds(twin * 128, 128)] = first.astype(BF16)
            mixed[slot, pl.ds(row + half_rows, ENS), pl.ds(twin * 128, 128)] = second.astype(BF16)
        return carry

    lax.fori_loop(0, PAIRS * PARTS, legendre_in, 0)
    for lane_block in range(DEGREES // 128):
        spectral[lane_block, pl.ds(ENTRIES * ENS, GROUPS * 8 * ENS - ENTRIES * ENS), :] = jnp.zeros(
            (GROUPS * 8 * ENS - ENTRIES * ENS, 128), F32
        )

    leg_load.wait()

    def analysis(slot, carry):
        value = jnp.dot(mixed[slot], leg[slot], preferred_element_type=F32)
        for field in range(FIELDS):
            for c in range(2):
                row = (field % 2) * half_rows + (c * PAIRS + field // 2) * ENS
                to = pl.multiple_of((field * PARTS + 2 * slot + c) * ENS, ENS)
                for lane_block in range(DEGREES // 128):
                    spectral[lane_block, pl.ds(to, ENS), :] = value[
                        row : row + ENS, lane_block * 128 : lane_block * 128 + 128
                    ]
        return carry

    lax.fori_loop(0, DEV_SLOTS, analysis, 0)

    first_slot = (q_me * ENS + e) * DEV_SLOTS
    slot_waves = [wnum[first_slot + s] for s in range(DEV_SLOTS)]

    def spectral_group(index, carry):
        group = index // (DEGREES // 128)
        lane_block = index - group * (DEGREES // 128)
        entry = group * 8 + lax.broadcasted_iota(jnp.int32, (8, 128), 0)
        slot = lax.rem(entry // 2, DEV_SLOTS)
        wave = jnp.where(slot == 0, slot_waves[0], jnp.where(slot == 1, slot_waves[1], slot_waves[2]))
        degree = lane_block * 128 + lax.broadcasted_iota(jnp.int32, (8, 128), 1)
        usable = jnp.logical_and(degree >= wave, degree <= LMAX)
        weight = jnp.where(usable, jnp.where(wave == 0, 1.0, 2.0), 0.0)
        base = group * (8 * ENS)
        x = jnp.stack(
            [spectral[lane_block, pl.ds(base + m, 8, stride=ENS), :] for m in range(ENS)], axis=0
        )
        x = jnp.where(usable[None], x, 0.0).astype(BF16).astype(F32)
        rows = pl.ds(pl.multiple_of(group * 8, 8), 8)
        y = tspec[rows, pl.ds(pl.multiple_of(lane_block * 128, 128), 128)]
        score, slope = crps_block(x, y)
        spec_sum[rows, :] = spec_sum[rows, :] + score * weight
        slope = slope * weight[None]
        for m in range(ENS):
            spectral[lane_block, pl.ds(base + m, 8, stride=ENS), :] = slope[m]
        return carry

    lax.fori_loop(0, GROUPS * (DEGREES // 128), spectral_group, 0)

    def synthesis(slot, carry):
        for field in range(FIELDS):
            for c in range(2):
                row = (field % 2) * half_rows + (c * PAIRS + field // 2) * ENS
                at = pl.multiple_of((field * PARTS + 2 * slot + c) * ENS, ENS)
                for lane_block in range(DEGREES // 128):
                    mixed[slot, pl.ds(row, ENS), pl.ds(lane_block * 128, 128)] = spectral[
                        lane_block, pl.ds(at, ENS), :
                    ].astype(BF16)
        value = lax.dot_general(
            mixed[slot, :, pl.ds(0, DEGREES)], leg[slot], (((1,), (1,)), ((), ())),
            preferred_element_type=F32,
        )
        for pair in range(PAIRS):
            for c in range(2):
                row = (c * PAIRS + pair) * ENS
                for twin in range(LATS // 2):
                    lanes = slice(twin * 128, twin * 128 + 128)
                    even, odd = swap(
                        value[row : row + ENS, lanes],
                        value[row + half_rows : row + half_rows + ENS, lanes],
                    )
                    start = (2 * slot + c) * PLANE + 2 * XS * twin
                    for i in range(XS):
                        members = slice(i * ZS, i * ZS + ZS)
                        wide[pair, pl.ds(start + i, ZS, stride=per_z), :] = even[members]
                        wide[pair, pl.ds(start + XS + i, ZS, stride=per_z), :] = odd[members]
        return carry

    lax.fori_loop(0, DEV_SLOTS, synthesis, 0)

    def narrow(index, carry):
        rows = pl.ds(pl.multiple_of(index * 48, 48), 48)
        for pair in range(PAIRS):
            send[rows, pl.ds(pair * 128, 128)] = wide[pair, rows, :].astype(BF16)
        return carry

    lax.fori_loop(0, COLS // 48, narrow, 0)
    exchange(z_copy, ZS, z_peer, z_me, per_z, got_c1, c1_send, c1_recv)
    d_start(0)
    grid_chunk(1)
    dx_start(1)
    d_start(1)
    d_forward(0)
    grid_chunk(2)
    dx_start(2)
    d_start(2)
    d_forward(1)

    lane = lax.broadcasted_iota(jnp.int32, (BAND, 128), 1)
    total = jnp.zeros((BAND, 128), F32)
    for local in range(3):
        rows_sum = jnp.sum(scores[local], axis=1, keepdims=True) * (1.0 / LON)
        total = total + jnp.where(lane == field_first + local, rows_sum, 0.0)
    score_sum[...] = total.reshape(LATS, 8, 128)

    def s_copy(peer, slot):
        return pltpu.make_async_remote_copy(
            src_ref=score_sum.at[peer // 2],
            dst_ref=got_s.at[slot],
            send_sem=s_send.at[peer],
            recv_sem=s_recv.at[slot],
            device_id={"ens": peer},
            device_id_type=MESH,
        )

    def s_start(k, carry):
        s_copy(ens_peer(k), e).start()
        return carry

    lax.fori_loop(1, ENS, s_start, 0)
    got_s[e] = score_sum[e // 2]

    d_forward(2)
    finish(z_copy, ZS, z_peer, z_me, got_c1, c1_send, c1_recv)
    widen(got_c1)

    def regroup_c(place, carry):
        rows = pl.ds(pl.multiple_of(place * per_plane, per_plane), per_plane)
        for pair in range(PAIRS):
            send[rows, pl.ds(pair * 128, 128)] = wide[
                pair, pl.ds(place, per_plane, stride=PLANE), :
            ].astype(BF16)
        return carry

    lax.fori_loop(0, PLANE, regroup_c, 0)
    exchange(plane_copy, PLANE, plane_peer, g_me, per_plane, got_c2, c2_send, c2_recv)
    sums = jnp.sum(spec_sum[...], axis=1, keepdims=True) * (1.0 / (2.0 * (LMAX + 1)))
    entry = lax.broadcasted_iota(jnp.int32, (GROUPS * 8, 128), 0)
    variables = FIELDS // BATCHES
    place = lax.broadcasted_iota(jnp.int32, (GROUPS * 8, 128), 1)
    sums = jnp.where(place == lax.rem(entry // PARTS, variables), sums, 0.0)
    for b in range(BATCHES):
        for slot in range(DEV_SLOTS):
            chosen = jnp.logical_and(
                entry // (PARTS * variables) == b, lax.rem(entry, PARTS) // 2 == slot
            )
            small[pl.ds(8 + b * DEV_SLOTS + slot, 1), :] = jnp.sum(
                jnp.where(chosen, sums, 0.0), axis=0, keepdims=True
            )
    finish(plane_copy, PLANE, plane_peer, g_me, got_c2, c2_send, c2_recv)

    def backward(index, carry):
        lanes = pl.ds(pl.multiple_of(index * 384, 384), 384)
        grad[lanes, :] = lax.dot_general(
            got_c2[:, lanes], table[...], (((0,), (0,)), ((), ())), preferred_element_type=F32
        )
        return carry

    lax.fori_loop(0, ROWS // 384, backward, 0)
    grad_store = pltpu.make_async_copy(grad, grad_hbm, grad_sem)
    grad_store.start()

    def s_wait(k, carry):
        s_copy(ens_peer(k), e).wait_send()
        s_copy(e, ens_peer(k)).wait_recv()
        return carry

    for chunk in range(len(CHUNKS)):
        a_done(chunk)
    for chunk in range(len(CHUNKS)):
        d_wait(chunk)
    lax.fori_loop(1, ENS, s_wait, 0)
    rows = jnp.sum(got_s[...], axis=0)
    small[pl.ds(0, 4), :] = jnp.where(lax.rem(e, 2) == 0, rows[:4], rows[4:])
    grad_store.wait()


def combine_kernel(got_d, grad, small, out, row_out, spec_out):
    variables = FIELDS // BATCHES

    @pl.when(pl.program_id(0) == 0)
    def _():
        for b in range(BATCHES):
            row_out[b] = small[pl.ds(0, 4), pl.ds(b * variables, variables)]
            spec_out[b] = small[pl.ds(8 + b * DEV_SLOTS, DEV_SLOTS), pl.ds(0, variables)]

    def combine(field, carry):
        top = pl.multiple_of(field * BAND, BAND)
        tail = got_d[field * FIELD_TILES + FIELD_TILES - 1].astype(F32)
        for block in range(BLOCKS):
            rows = pl.ds(top + 16 * block, 16)
            for lane_block in range(FULL):
                lanes = pl.ds(lane_block * 128, 128)
                slope = got_d[field * FIELD_TILES + block * FULL + lane_block].astype(F32)
                out[rows, lanes] = (grad[rows, lanes] + slope).astype(BF16)
            lanes = pl.ds(FULL * 128, TAIL)
            moved = tail if block == 0 else pltpu.roll(tail, 128 - block * TAIL, 1)
            out[rows, lanes] = (grad[rows, lanes] + moved[:, :TAIL]).astype(BF16)
        return carry

    lax.fori_loop(0, FIELDS // STEPS, combine, 0)


def body(members, target, target_spectrum, legendre, wavenum):
    chunks = len(CHUNKS)
    vmem = pl.BlockSpec(memory_space=pltpu.VMEM)
    hbm = pl.BlockSpec(memory_space=pl.ANY)
    dma = pltpu.SemaphoreType.DMA
    slopes, grad, small = pl.pallas_call(
        body_kernel,
        out_shape=(
            jax.ShapeDtypeStruct((ENS * OWN, 16, 128), BF16),
            jax.ShapeDtypeStruct((ROWS, LON), F32),
            jax.ShapeDtypeStruct((24, 128), F32),
        ),
        in_specs=[hbm, hbm, vmem, hbm, vmem, pl.BlockSpec(memory_space=pltpu.SMEM)],
        out_specs=(hbm, hbm, vmem),
        scratch_shapes=[
            pltpu.VMEM((ROWS, LON), BF16),
            pltpu.VMEM((ROWS, LON), BF16),
            pltpu.VMEM((DEV_SLOTS, LATITUDES, DEGREES), BF16),
            pltpu.VMEM((ENS * OWN, 16, 128), BF16),
            pltpu.VMEM((OWN, 16, 128), F32),
            pltpu.VMEM((ENS, OWN, 16, 128), BF16),
            pltpu.VMEM((ZS, OWN, 16, 128), BF16),
            pltpu.VMEM((ZS, OWN, 16, 128), BF16),
            pltpu.VMEM((ROWS, LON), F32),
            pltpu.VMEM((COLS, LON), BF16),
            pltpu.VMEM((COLS, ROWS), BF16),
            pltpu.VMEM((COLS, ROWS), BF16),
            pltpu.VMEM((COLS, ROWS), BF16),
            pltpu.VMEM((COLS, ROWS), BF16),
            pltpu.VMEM((COLS, ROWS), BF16),
            pltpu.VMEM((PAIRS, COLS, 128), F32),
            pltpu.VMEM((DEV_SLOTS, FIELDS * 2 * ENS, LATITUDES), BF16),
            pltpu.VMEM((DEGREES // 128, GROUPS * 8 * ENS, 128), F32),
            pltpu.VMEM((GROUPS * 8, DEGREES), F32),
            pltpu.VMEM((GROUPS * 8, 128), F32),
            pltpu.VMEM((16, 128), F32),
            pltpu.VMEM((ENS, 16, 128), F32),
            pltpu.VMEM((ENS, 16, 128), F32),
            pltpu.VMEM((3, BAND, 128), F32),
            pltpu.VMEM((LATS, 8, 128), F32),
            pltpu.VMEM((ENS, 8, 128), F32),
            dma((chunks, ZS)), dma((chunks, ZS)),
            dma((chunks, ZS)), dma((chunks, ZS)),
            dma((chunks, ENS)), dma((chunks, ENS)),
            dma((chunks, ENS)), dma((chunks, ENS)),
            dma((PLANE,)), dma((PLANE,)),
            dma((ZS,)), dma((ZS,)),
            dma((ZS,)), dma((ZS,)),
            dma((PLANE,)), dma((PLANE,)),
            dma((ENS,)), dma((ENS,)),
            dma((LOADS,)), dma, dma, dma, dma((chunks, 2)),
        ],
        compiler_params=pltpu.CompilerParams(
            collective_id=0, has_side_effects=True, vmem_limit_bytes=60 * 2**20
        ),
    )(
        members.reshape(ROWS, LON),
        target.reshape(ROWS, LON),
        target_spectrum,
        legendre,
        wavenum.reshape(SLOTS // 128, 128),
        wavenum,
    )
    variables = FIELDS // BATCHES
    step_rows = ROWS // STEPS
    member_grad, row_score, spec_score = pl.pallas_call(
        combine_kernel,
        grid=(STEPS,),
        out_shape=(
            jax.ShapeDtypeStruct((ROWS, LON), BF16),
            jax.ShapeDtypeStruct((BATCHES, 4, variables), F32),
            jax.ShapeDtypeStruct((BATCHES, DEV_SLOTS, variables), F32),
        ),
        in_specs=[
            pl.BlockSpec((TILES // STEPS, 16, 128), lambda i: (i, 0, 0)),
            pl.BlockSpec((step_rows, LON), lambda i: (i, 0)),
            pl.BlockSpec((24, 128), lambda i: (0, 0)),
        ],
        out_specs=(
            pl.BlockSpec((step_rows, LON), lambda i: (i, 0)),
            pl.BlockSpec((BATCHES, 4, variables), lambda i: (0, 0, 0)),
            pl.BlockSpec((BATCHES, DEV_SLOTS, variables), lambda i: (0, 0, 0)),
        ),
        compiler_params=pltpu.CompilerParams(vmem_limit_bytes=32 * 2**20),
    )(slopes, grad, small)
    return (
        member_grad.reshape(members.shape),
        row_score.transpose(0, 2, 1),
        spec_score.transpose(0, 2, 1),
    )


def solution(mesh):
    in_specs = (
        P("ens", None, "var", "lat", None),
        P(None, "var", "lat", None),
        P(None, "var", ("lat", "ens"), None, None),
        P(("lat", "ens"), None, None),
        P(),
    )
    out_specs = (
        P("ens", None, "var", "lat", None),
        P(None, "var", ("lat", "ens")),
        P(None, "var", ("lat", "ens")),
    )
    return jax.shard_map(body, mesh=mesh, in_specs=in_specs, out_specs=out_specs, check_vma=False)
```

```python
import functools
import math

import jax
import jax.numpy as jnp
from jax import lax
from jax.experimental import pallas as pl
from jax.experimental.pallas import tpu as pltpu
from jax.sharding import PartitionSpec as P

LMAX = 360
MESH = pl.DeviceIdType.MESH
F32 = jnp.float32
BF16 = jnp.bfloat16
WIDTH2 = 0.0625

ENS = 16
ZS = 8
XS = 2
LATS = 8
PLANE = LATS * XS
FIELDS = 18
BATCHES = 3
BAND = 64
ROWS = FIELDS * BAND
LON = 1440
SLOTS = 384
COLS = 2 * SLOTS
DEV_SLOTS = 3
PARTS = 2 * DEV_SLOTS
LATITUDES = 512
DEGREES = 384
PAIRS = FIELDS // 2
FULL = LON // 128
TAIL = LON - FULL * 128
BLOCKS = BAND // 16
FIELD_TILES = BLOCKS * FULL + 1
TILES = FIELDS * FIELD_TILES
OWN = -(-TILES // ENS)
CHUNKS = ((0, 9), (9, 18), (27, 24))
LOADS = 3
STEPS = 6
ENTRIES = FIELDS * PARTS
GROUPS = -(-ENTRIES // 8)


def crps_block(x, y):
    offset = x - y[None]
    square = offset * offset + WIDTH2
    inverse = lax.rsqrt(square)
    near = jnp.sum(square * inverse, axis=0)
    slope = jnp.zeros_like(x)
    spread = jnp.zeros_like(y)
    half = ENS // 2
    for shift in range(1, half):
        d = x - jnp.concatenate([x[shift:], x[:shift]], axis=0)
        s = d * d + WIDTH2
        r = lax.rsqrt(s)
        spread = spread + jnp.sum(s * r, axis=0)
        ratio = d * r
        back = jnp.concatenate([ratio[ENS - shift:], ratio[: ENS - shift]], axis=0)
        slope = slope + (ratio - back)
    d = x[:half] - x[half:]
    s = d * d + WIDTH2
    r = lax.rsqrt(s)
    spread = spread + jnp.sum(s * r, axis=0)
    ratio = d * r
    slope = slope + jnp.concatenate([ratio, -ratio], axis=0)
    pair_mean = (2.0 * spread + ENS * math.sqrt(WIDTH2)) * (0.5 / (ENS * ENS))
    return near * (1.0 / ENS) - pair_mean, offset * inverse - slope * (1.0 / ENS)


def body_kernel(
    mem_hbm, tgt_hbm, tsp, leg_hbm, wave_rows, wnum,
    got_d, grad, small,
    mem, tgt, leg, tiles, own_target, got_a, stage_a, stage_d, table, send, got_b1, got_b2, got_c1, got_c2,
    wide, mixed, spectral, tspec, spec_sum, part, xs, ys, scores, score_sum, got_s,
    ax_send, ax_recv, dx_send, dx_recv, a_send, a_recv, d_send, d_recv, b1_send, b1_recv, b2_send, b2_recv,
    c1_send, c1_recv, c2_send, c2_recv, s_send, s_recv, mem_sem, tgt_sem, leg_sem, keep_sem,
):
    e = lax.axis_index("ens")
    q_me = lax.axis_index("lat")

    def ens_peer(k):
        return lax.rem(e + k, ENS)

    x_me = e // ZS
    z_me = e - x_me * ZS
    partner = (1 - x_me) * ZS + z_me
    g_me = q_me * XS + x_me

    def z_peer(k):
        return lax.rem(z_me + k, ZS)

    def plane_peer(k):
        return lax.rem(g_me + k, PLANE)

    def mem_load(index):
        rows = pl.ds(index * (ROWS // LOADS), ROWS // LOADS)
        return pltpu.make_async_copy(mem_hbm.at[rows], mem.at[rows], mem_sem.at[index])

    tgt_load = pltpu.make_async_copy(tgt_hbm, tgt, tgt_sem)
    leg_load = pltpu.make_async_copy(leg_hbm, leg, leg_sem)
    for index in range(LOADS):
        mem_load(index).start()
    tgt_load.start()
    leg_load.start()
    barrier = pltpu.get_barrier_semaphore()

    def greet_ens(k, carry):
        pl.semaphore_signal(barrier, inc=1, device_id={"ens": ens_peer(k)}, device_id_type=MESH)
        return carry

    def greet_plane(k, carry):
        for x in range(XS):
            pl.semaphore_signal(
                barrier,
                inc=1,
                device_id={"ens": x * ZS + z_me, "lat": lax.rem(q_me + k, LATS)},
                device_id_type=MESH,
            )
        return carry

    lax.fori_loop(1, ENS, greet_ens, 0)
    lax.fori_loop(1, LATS, greet_plane, 0)

    def retile(field, carry):
        rows = pl.multiple_of(field * BAND, BAND)
        for block in range(BLOCKS):
            for lane in range(FULL):
                tiles[field * FIELD_TILES + block * FULL + lane] = mem[
                    pl.ds(rows + 16 * block, 16), pl.ds(lane * 128, 128)
                ]
        tails = [
            mem[pl.ds(rows + 16 * block, 16), pl.ds(FULL * 128, TAIL)].astype(F32)
            for block in range(BLOCKS)
        ]
        tiles[field * FIELD_TILES + FIELD_TILES - 1] = jnp.concatenate(tails, axis=1).astype(BF16)
        return carry

    for index in range(LOADS):
        mem_load(index).wait()
        lax.fori_loop(index * (FIELDS // LOADS), (index + 1) * (FIELDS // LOADS), retile, 0)
    tiles[pl.ds(TILES, ENS * OWN - TILES)] = jnp.zeros((ENS * OWN - TILES, 16, 128), BF16)

    def ax_copy(chunk, z):
        first, count = CHUNKS[chunk]
        return pltpu.make_async_remote_copy(
            src_ref=tiles.at[pl.ds(((1 - x_me) * ZS + z) * OWN + first, count)],
            dst_ref=stage_a.at[z, pl.ds(first, count)],
            send_sem=ax_send.at[chunk, z],
            recv_sem=ax_recv.at[chunk, z],
            device_id={"ens": partner},
            device_id_type=MESH,
        )

    def a_copy(chunk, z, slot):
        first, count = CHUNKS[chunk]
        return pltpu.make_async_remote_copy(
            src_ref=tiles.at[pl.ds((x_me * ZS + z) * OWN + first, count)],
            dst_ref=got_a.at[slot, pl.ds(first, count)],
            send_sem=a_send.at[chunk, z],
            recv_sem=a_recv.at[chunk, slot],
            device_id={"ens": x_me * ZS + z},
            device_id_type=MESH,
        )

    def a_pass(chunk, z, slot):
        first, count = CHUNKS[chunk]
        return pltpu.make_async_remote_copy(
            src_ref=stage_a.at[z, pl.ds(first, count)],
            dst_ref=got_a.at[slot, pl.ds(first, count)],
            send_sem=a_send.at[chunk, ZS + z],
            recv_sem=a_recv.at[chunk, slot],
            device_id={"ens": x_me * ZS + z},
            device_id_type=MESH,
        )

    def ax_start(chunk):
        def step(k, carry):
            ax_copy(chunk, z_peer(k)).start()
            return carry

        lax.fori_loop(1, ZS + 1, step, 0)

    def a_start(chunk):
        def step(k, carry):
            a_copy(chunk, z_peer(k), e).start()
            return carry

        lax.fori_loop(1, ZS, step, 0)
        first, count = CHUNKS[chunk]
        got_a[e, pl.ds(first, count)] = tiles[pl.ds(e * OWN + first, count)]

    def a_forward(chunk):
        def step(k, carry):
            ax_copy(chunk, z_peer(k)).wait_recv()
            a_pass(chunk, z_peer(k), partner).start()
            return carry

        lax.fori_loop(1, ZS, step, 0)
        ax_copy(chunk, z_me).wait_recv()
        first, count = CHUNKS[chunk]
        got_a[partner, pl.ds(first, count)] = stage_a[z_me, pl.ds(first, count)]

    def a_wait(chunk):
        def step(k, carry):
            a_copy(chunk, z_me, x_me * ZS + z_peer(k)).wait_recv()
            a_pass(chunk, z_me, (1 - x_me) * ZS + z_peer(k)).wait_recv()
            return carry

        lax.fori_loop(1, ZS, step, 0)

    def a_done(chunk):
        def step(k, carry):
            a_copy(chunk, z_peer(k), e).wait_send()
            a_pass(chunk, z_peer(k), partner).wait_send()
            return carry

        def step_x(z, carry):
            ax_copy(chunk, z).wait_send()
            return carry

        lax.fori_loop(1, ZS, step, 0)
        lax.fori_loop(0, ZS, step_x, 0)

    pl.semaphore_wait(barrier, ENS - 1 + XS * (LATS - 1))
    for chunk in range(len(CHUNKS)):
        a_start(chunk)
        if chunk == 0:
            ax_start(0)

    def table_rows(index, carry):
        rows = pl.ds(pl.multiple_of(index * 64, 64), 64)
        lane = lax.broadcasted_iota(jnp.int32, (64, 128), 1).astype(F32)
        row = lax.broadcasted_iota(jnp.int32, (64, 128), 0)
        group = wave_rows[pl.ds(index // 4, 1), :].astype(F32)
        at = lax.rem(index, 4) * 32 + row // 2
        wave = jnp.sum(
            jnp.where(lax.broadcasted_iota(jnp.int32, (64, 128), 1) == at, group, 0.0),
            axis=1,
            keepdims=True,
        )

        def angles(turns):
            turns = turns - LON * jnp.floor(turns * (1.0 / LON))
            return turns * (2.0 * math.pi / LON)

        fine = angles(wave * lane)
        coarse = angles(wave * (128.0 * jnp.minimum(lane, 15.0)))
        cos_b, sin_b = jnp.cos(fine), jnp.sin(fine)
        factor = 1.0 / math.sqrt(LON)
        cos_a, sin_a = jnp.cos(coarse) * factor, jnp.sin(coarse) * factor
        real = lax.rem(row, 2) == 0
        first = jnp.where(real, cos_a, -sin_a)
        second = jnp.where(real, -sin_a, -cos_a)
        for lane_block in range(FULL + 1):
            width = min(128, LON - lane_block * 128)
            value = first[:, lane_block : lane_block + 1] * cos_b
            value = value + second[:, lane_block : lane_block + 1] * sin_b
            table[rows, pl.ds(lane_block * 128, width)] = value[:, :width].astype(BF16)
        return carry

    lax.fori_loop(0, COLS // 64, table_rows, 0)

    def forward(index, carry):
        lanes = pl.ds(pl.multiple_of(index * 384, 384), 384)
        value = lax.dot_general(
            table[...], mem[lanes, :], (((1,), (1,)), ((), ())), preferred_element_type=F32
        )
        send[:, lanes] = value.astype(BF16)
        return carry

    lax.fori_loop(0, ROWS // 384, forward, 0)

    per_plane = COLS // PLANE
    per_z = COLS // ZS

    def plane_copy(source, got, s_sem, r_sem, peer, slot):
        return pltpu.make_async_remote_copy(
            src_ref=source.at[pl.ds(peer * per_plane, per_plane)],
            dst_ref=got.at[pl.ds(slot * per_plane, per_plane)],
            send_sem=s_sem.at[peer],
            recv_sem=r_sem.at[slot],
            device_id={"ens": lax.rem(peer, XS) * ZS + z_me, "lat": peer // XS},
            device_id_type=MESH,
        )

    def z_copy(source, got, s_sem, r_sem, peer, slot):
        return pltpu.make_async_remote_copy(
            src_ref=source.at[pl.ds(peer * per_z, per_z)],
            dst_ref=got.at[pl.ds(slot * per_z, per_z)],
            send_sem=s_sem.at[peer],
            recv_sem=r_sem.at[slot],
            device_id={"ens": x_me * ZS + peer},
            device_id_type=MESH,
        )

    def exchange(copy, count, peer_of, me, size, got, s_sem, r_sem):
        def start(k, carry):
            copy(send, got, s_sem, r_sem, peer_of(k), me).start()
            return carry

        lax.fori_loop(1, count, start, 0)
        mine = pl.ds(pl.multiple_of(me * size, size), size)
        got[mine, :] = send[mine, :]

    def finish_near(copy, count, peer_of, me, got, s_sem, r_sem):
        for k in (1, count - 1, 2, count - 2):
            copy(send, got, s_sem, r_sem, me, peer_of(k)).wait_recv()

    def finish_far(copy, count, peer_of, me, got, s_sem, r_sem):
        for k in range(3, count - 2):
            copy(send, got, s_sem, r_sem, me, peer_of(k)).wait_recv()
        for k in range(1, count):
            copy(send, got, s_sem, r_sem, peer_of(k), me).wait_send()

    def finish(copy, count, peer_of, me, got, s_sem, r_sem):
        def wait(k, carry):
            copy(send, got, s_sem, r_sem, peer_of(k), me).wait_send()
            copy(send, got, s_sem, r_sem, me, peer_of(k)).wait_recv()
            return carry

        lax.fori_loop(1, count, wait, 0)

    def widen(got):
        def step(index, carry):
            rows = pl.ds(pl.multiple_of(index * 48, 48), 48)
            for pair in range(PAIRS):
                wide[pair, rows, :] = got[rows, pl.ds(pair * 128, 128)].astype(F32)
            return carry

        lax.fori_loop(0, COLS // 48, step, 0)

    exchange(plane_copy, PLANE, plane_peer, g_me, per_plane, got_b1, b1_send, b1_recv)

    tgt_load.wait()

    def target_tile(index, carry):
        tile = e * OWN + index
        field = tile // FIELD_TILES
        place = tile - field * FIELD_TILES

        @pl.when(jnp.logical_and(place < FIELD_TILES - 1, tile < TILES))
        def _():
            block = place // FULL
            lane = place - block * FULL
            rows = pl.multiple_of(field * BAND + block * 16, 16)
            own_target[index] = tgt[
                pl.ds(rows, 16), pl.ds(pl.multiple_of(lane * 128, 128), 128)
            ].astype(F32)

        @pl.when(jnp.logical_and(place == FIELD_TILES - 1, tile < TILES))
        def _():
            rows = pl.multiple_of(field * BAND, BAND)
            tails = [
                tgt[pl.ds(rows + 16 * block, 16), pl.ds(FULL * 128, TAIL)].astype(F32)
                for block in range(BLOCKS)
            ]
            own_target[index] = jnp.concatenate(tails, axis=1)

        @pl.when(tile >= TILES)
        def _():
            own_target[index] = jnp.zeros((16, 128), F32)

        return carry

    lax.fori_loop(0, OWN, target_tile, 0)
    field_first = (e * OWN) // FIELD_TILES
    scores[...] = jnp.zeros_like(scores)
    for b in range(BATCHES):
        for v in range(FIELDS // BATCHES):
            for s in range(DEV_SLOTS):
                row = (b * (FIELDS // BATCHES) + v) * PARTS + 2 * s
                tspec[pl.ds(row, 2), :] = tsp[b, v, s].astype(F32)
    tspec[pl.ds(ENTRIES, GROUPS * 8 - ENTRIES), :] = jnp.zeros((GROUPS * 8 - ENTRIES, DEGREES), F32)
    spec_sum[...] = jnp.zeros_like(spec_sum)

    a_forward(0)
    finish(plane_copy, PLANE, plane_peer, g_me, got_b1, b1_send, b1_recv)
    widen(got_b1)

    def regroup_b(peer, carry):
        for pair in range(PAIRS):
            for piece in range(PARTS):
                value = wide[pair, pl.ds(peer * PARTS + piece, PLANE, stride=per_plane), :]
                rows = pl.multiple_of(peer * per_z + PLANE * piece, PLANE)
                send[pl.ds(rows, PLANE), pl.ds(pair * 128, 128)] = value.astype(BF16)
        return carry

    lax.fori_loop(0, ZS, regroup_b, 0)
    exchange(z_copy, ZS, z_peer, z_me, per_z, got_b2, b2_send, b2_recv)
    ax_start(1)
    ax_start(2)

    def grid_tile(index, carry):
        def load(member, inner):
            xs[member] = got_a[member, index].astype(F32)
            return inner

        lax.fori_loop(0, ENS, load, 0, unroll=True)
        for top in (0, 8):
            rows = pl.ds(top, 8)
            score, slope = crps_block(xs[:, rows, :], own_target[index, rows, :])
            ys[:, rows, :] = slope
            part[rows, :] = score

        def store(member, inner):
            got_a[member, index] = ys[member].astype(BF16)
            return inner

        lax.fori_loop(0, ENS, store, 0, unroll=True)
        tile = e * OWN + index
        field = tile // FIELD_TILES
        place = tile - field * FIELD_TILES
        local = field - field_first

        @pl.when(place < FIELD_TILES - 1)
        def _():
            rows = pl.ds(pl.multiple_of(place // FULL * 16, 16), 16)
            scores[local, rows, :] = scores[local, rows, :] + part[...]

        @pl.when(place == FIELD_TILES - 1)
        def _():
            segment = lax.broadcasted_iota(jnp.int32, (16, 128), 1) // TAIL
            for block in range(BLOCKS):
                rows = pl.ds(16 * block, 16)
                scores[local, rows, :] = scores[local, rows, :] + jnp.where(
                    segment == block, part[...], 0.0
                )

        return carry

    def dx_copy(chunk, z):
        first, count = CHUNKS[chunk]
        return pltpu.make_async_remote_copy(
            src_ref=got_a.at[(1 - x_me) * ZS + z, pl.ds(first, count)],
            dst_ref=stage_d.at[z, pl.ds(first, count)],
            send_sem=dx_send.at[chunk, z],
            recv_sem=dx_recv.at[chunk, z],
            device_id={"ens": partner},
            device_id_type=MESH,
        )

    def d_copy(chunk, z, slot):
        first, count = CHUNKS[chunk]
        return pltpu.make_async_remote_copy(
            src_ref=got_a.at[x_me * ZS + z, pl.ds(first, count)],
            dst_ref=got_d.at[pl.ds(slot * OWN + first, count)],
            send_sem=d_send.at[chunk, z],
            recv_sem=d_recv.at[chunk, slot],
            device_id={"ens": x_me * ZS + z},
            device_id_type=MESH,
        )

    def d_pass(chunk, z, slot):
        first, count = CHUNKS[chunk]
        return pltpu.make_async_remote_copy(
            src_ref=stage_d.at[z, pl.ds(first, count)],
            dst_ref=got_d.at[pl.ds(slot * OWN + first, count)],
            send_sem=d_send.at[chunk, ZS + z],
            recv_sem=d_recv.at[chunk, slot],
            device_id={"ens": x_me * ZS + z},
            device_id_type=MESH,
        )

    def d_keep(chunk):
        first, count = CHUNKS[chunk]
        return pltpu.make_async_copy(
            got_a.at[e, pl.ds(first, count)],
            got_d.at[pl.ds(e * OWN + first, count)],
            keep_sem.at[chunk, 0],
        )

    def d_cross(chunk):
        first, count = CHUNKS[chunk]
        return pltpu.make_async_copy(
            stage_d.at[z_me, pl.ds(first, count)],
            got_d.at[pl.ds(partner * OWN + first, count)],
            keep_sem.at[chunk, 1],
        )

    def dx_start(chunk):
        def step(k, carry):
            dx_copy(chunk, z_peer(k)).start()
            return carry

        lax.fori_loop(1, ZS + 1, step, 0)

    def d_start(chunk):
        def step(k, carry):
            d_copy(chunk, z_peer(k), e).start()
            return carry

        lax.fori_loop(1, ZS, step, 0)
        d_keep(chunk).start()

    def d_forward(chunk):
        def step(k, carry):
            dx_copy(chunk, z_peer(k)).wait_recv()
            d_pass(chunk, z_peer(k), partner).start()
            return carry

        lax.fori_loop(1, ZS, step, 0)
        dx_copy(chunk, z_me).wait_recv()
        d_cross(chunk).start()

    def d_wait(chunk):
        def step(k, carry):
            d_copy(chunk, z_peer(k), e).wait_send()
            d_pass(chunk, z_peer(k), partner).wait_send()
            d_copy(chunk, z_me, x_me * ZS + z_peer(k)).wait_recv()
            d_pass(chunk, z_me, (1 - x_me) * ZS + z_peer(k)).wait_recv()
            return carry

        def step_x(z, carry):
            dx_copy(chunk, z).wait_send()
            return carry

        lax.fori_loop(1, ZS, step, 0)
        lax.fori_loop(0, ZS, step_x, 0)
        d_keep(chunk).wait()
        d_cross(chunk).wait()

    def grid_chunk(chunk):
        a_wait(chunk)
        first, count = CHUNKS[chunk]
        lax.fori_loop(first, first + count, grid_tile, 0)

    grid_chunk(0)
    dx_start(0)

    finish_near(z_copy, ZS, z_peer, z_me, got_b2, b2_send, b2_recv)
    a_forward(1)
    finish_far(z_copy, ZS, z_peer, z_me, got_b2, b2_send, b2_recv)
    a_forward(2)
    widen(got_b2)
    low = lax.broadcasted_iota(jnp.int32, (16, 128), 1) < 64

    def swap(even, odd):
        first = jnp.where(low, even, pltpu.roll(odd, 64, 1))
        second = jnp.where(low, pltpu.roll(even, 64, 1), odd)
        return first, second

    half_rows = 2 * PAIRS * ENS

    def legendre_in(index, carry):
        pair = index // PARTS
        piece = index - pair * PARTS
        slot = piece // 2
        c = piece - 2 * slot
        row = pl.multiple_of((c * PAIRS + pair) * ENS, ENS)
        for twin in range(LATS // 2):
            start = piece * PLANE + 2 * XS * twin
            rows = [wide[pair, pl.ds(start + i, ZS, stride=per_z), :] for i in range(2 * XS)]
            even = jnp.concatenate(rows[:XS], axis=0)
            odd = jnp.concatenate(rows[XS:], axis=0)
            first, second = swap(even, odd)
            mixed[slot, pl.ds(row, ENS), pl.ds(twin * 128, 128)] = first.astype(BF16)
            mixed[slot, pl.ds(row + half_rows, ENS), pl.ds(twin * 128, 128)] = second.astype(BF16)
        return carry

    lax.fori_loop(0, PAIRS * PARTS, legendre_in, 0)
    for lane_block in range(DEGREES // 128):
        spectral[lane_block, pl.ds(ENTRIES * ENS, GROUPS * 8 * ENS - ENTRIES * ENS), :] = jnp.zeros(
            (GROUPS * 8 * ENS - ENTRIES * ENS, 128), F32
        )

    leg_load.wait()

    def analysis(slot, carry):
        value = jnp.dot(mixed[slot], leg[slot], preferred_element_type=F32)
        for field in range(FIELDS):
            for c in range(2):
                row = (field % 2) * half_rows + (c * PAIRS + field // 2) * ENS
                to = pl.multiple_of((field * PARTS + 2 * slot + c) * ENS, ENS)
                for lane_block in range(DEGREES // 128):
                    spectral[lane_block, pl.ds(to, ENS), :] = value[
                        row : row + ENS, lane_block * 128 : lane_block * 128 + 128
                    ]
        return carry

    lax.fori_loop(0, DEV_SLOTS, analysis, 0)

    first_slot = (q_me * ENS + e) * DEV_SLOTS
    slot_waves = [wnum[first_slot + s] for s in range(DEV_SLOTS)]

    def spectral_group(index, carry):
        group = index // (DEGREES // 128)
        lane_block = index - group * (DEGREES // 128)
        entry = group * 8 + lax.broadcasted_iota(jnp.int32, (8, 128), 0)
        slot = lax.rem(entry // 2, DEV_SLOTS)
        wave = jnp.where(slot == 0, slot_waves[0], jnp.where(slot == 1, slot_waves[1], slot_waves[2]))
        degree = lane_block * 128 + lax.broadcasted_iota(jnp.int32, (8, 128), 1)
        usable = jnp.logical_and(degree >= wave, degree <= LMAX)
        weight = jnp.where(usable, jnp.where(wave == 0, 1.0, 2.0), 0.0)
        base = group * (8 * ENS)
        x = jnp.stack(
            [spectral[lane_block, pl.ds(base + m, 8, stride=ENS), :] for m in range(ENS)], axis=0
        )
        x = jnp.where(usable[None], x, 0.0).astype(BF16).astype(F32)
        rows = pl.ds(pl.multiple_of(group * 8, 8), 8)
        y = tspec[rows, pl.ds(pl.multiple_of(lane_block * 128, 128), 128)]
        score, slope = crps_block(x, y)
        spec_sum[rows, :] = spec_sum[rows, :] + score * weight
        slope = slope * weight[None]
        for m in range(ENS):
            spectral[lane_block, pl.ds(base + m, 8, stride=ENS), :] = slope[m]
        return carry

    lax.fori_loop(0, GROUPS * (DEGREES // 128), spectral_group, 0)

    def synthesis(slot, carry):
        for field in range(FIELDS):
            for c in range(2):
                row = (field % 2) * half_rows + (c * PAIRS + field // 2) * ENS
                at = pl.multiple_of((field * PARTS + 2 * slot + c) * ENS, ENS)
                for lane_block in range(DEGREES // 128):
                    mixed[slot, pl.ds(row, ENS), pl.ds(lane_block * 128, 128)] = spectral[
                        lane_block, pl.ds(at, ENS), :
                    ].astype(BF16)
        value = lax.dot_general(
            mixed[slot, :, pl.ds(0, DEGREES)], leg[slot], (((1,), (1,)), ((), ())),
            preferred_element_type=F32,
        )
        for pair in range(PAIRS):
            for c in range(2):
                row = (c * PAIRS + pair) * ENS
                for twin in range(LATS // 2):
                    lanes = slice(twin * 128, twin * 128 + 128)
                    even, odd = swap(
                        value[row : row + ENS, lanes],
                        value[row + half_rows : row + half_rows + ENS, lanes],
                    )
                    start = (2 * slot + c) * PLANE + 2 * XS * twin
                    for i in range(XS):
                        members = slice(i * ZS, i * ZS + ZS)
                        wide[pair, pl.ds(start + i, ZS, stride=per_z), :] = even[members]
                        wide[pair, pl.ds(start + XS + i, ZS, stride=per_z), :] = odd[members]
        return carry

    lax.fori_loop(0, DEV_SLOTS, synthesis, 0)

    def narrow(index, carry):
        rows = pl.ds(pl.multiple_of(index * 48, 48), 48)
        for pair in range(PAIRS):
            send[rows, pl.ds(pair * 128, 128)] = wide[pair, rows, :].astype(BF16)
        return carry

    lax.fori_loop(0, COLS // 48, narrow, 0)
    exchange(z_copy, ZS, z_peer, z_me, per_z, got_c1, c1_send, c1_recv)
    grid_chunk(1)
    dx_start(1)
    grid_chunk(2)
    dx_start(2)
    finish_near(z_copy, ZS, z_peer, z_me, got_c1, c1_send, c1_recv)
    d_start(0)
    d_forward(0)

    lane = lax.broadcasted_iota(jnp.int32, (BAND, 128), 1)
    total = jnp.zeros((BAND, 128), F32)
    for local in range(3):
        rows_sum = jnp.sum(scores[local], axis=1, keepdims=True) * (1.0 / LON)
        total = total + jnp.where(lane == field_first + local, rows_sum, 0.0)
    score_sum[...] = total.reshape(LATS, 8, 128)

    def s_copy(peer, slot):
        return pltpu.make_async_remote_copy(
            src_ref=score_sum.at[peer // 2],
            dst_ref=got_s.at[slot],
            send_sem=s_send.at[peer],
            recv_sem=s_recv.at[slot],
            device_id={"ens": peer},
            device_id_type=MESH,
        )

    def s_start(k, carry):
        s_copy(ens_peer(k), e).start()
        return carry

    lax.fori_loop(1, ENS, s_start, 0)
    got_s[e] = score_sum[e // 2]

    finish_far(z_copy, ZS, z_peer, z_me, got_c1, c1_send, c1_recv)
    d_start(1)
    d_forward(1)
    d_start(2)
    d_forward(2)
    widen(got_c1)

    def regroup_c(place, carry):
        rows = pl.ds(pl.multiple_of(place * per_plane, per_plane), per_plane)
        for pair in range(PAIRS):
            send[rows, pl.ds(pair * 128, 128)] = wide[
                pair, pl.ds(place, per_plane, stride=PLANE), :
            ].astype(BF16)
        return carry

    lax.fori_loop(0, PLANE, regroup_c, 0)
    exchange(plane_copy, PLANE, plane_peer, g_me, per_plane, got_c2, c2_send, c2_recv)
    sums = jnp.sum(spec_sum[...], axis=1, keepdims=True) * (1.0 / (2.0 * (LMAX + 1)))
    entry = lax.broadcasted_iota(jnp.int32, (GROUPS * 8, 128), 0)
    variables = FIELDS // BATCHES
    place = lax.broadcasted_iota(jnp.int32, (GROUPS * 8, 128), 1)
    sums = jnp.where(place == lax.rem(entry // PARTS, variables), sums, 0.0)
    for b in range(BATCHES):
        for slot in range(DEV_SLOTS):
            chosen = jnp.logical_and(
                entry // (PARTS * variables) == b, lax.rem(entry, PARTS) // 2 == slot
            )
            small[pl.ds(8 + b * DEV_SLOTS + slot, 1), :] = jnp.sum(
                jnp.where(chosen, sums, 0.0), axis=0, keepdims=True
            )
    finish(plane_copy, PLANE, plane_peer, g_me, got_c2, c2_send, c2_recv)

    def backward(index, carry):
        lanes = pl.ds(pl.multiple_of(index * 384, 384), 384)
        grad[lanes, :] = lax.dot_general(
            got_c2[:, lanes], table[...], (((0,), (0,)), ((), ())), preferred_element_type=F32
        )
        return carry

    lax.fori_loop(0, ROWS // 384, backward, 0)

    def s_wait(k, carry):
        s_copy(ens_peer(k), e).wait_send()
        s_copy(e, ens_peer(k)).wait_recv()
        return carry

    for chunk in range(len(CHUNKS)):
        a_done(chunk)
    for chunk in range(len(CHUNKS)):
        d_wait(chunk)
    lax.fori_loop(1, ENS, s_wait, 0)
    rows = jnp.sum(got_s[...], axis=0)
    small[pl.ds(0, 4), :] = jnp.where(lax.rem(e, 2) == 0, rows[:4], rows[4:])


def combine_kernel(got_d, grad, small, out_hbm, row_out, spec_out, out, out_sem):
    variables = FIELDS // BATCHES
    for b in range(BATCHES):
        row_out[b] = small[pl.ds(0, 4), pl.ds(b * variables, variables)]
        spec_out[b] = small[pl.ds(8 + b * DEV_SLOTS, DEV_SLOTS), pl.ds(0, variables)]

    def combine(field, carry):
        top = pl.multiple_of(field * BAND, BAND)
        tail = got_d[field * FIELD_TILES + FIELD_TILES - 1].astype(F32)
        for block in range(BLOCKS):
            rows = pl.ds(top + 16 * block, 16)
            for lane_block in range(FULL):
                lanes = pl.ds(lane_block * 128, 128)
                slope = got_d[field * FIELD_TILES + block * FULL + lane_block].astype(F32)
                out[rows, lanes] = (grad[rows, lanes] + slope).astype(BF16)
            lanes = pl.ds(FULL * 128, TAIL)
            moved = tail if block == 0 else pltpu.roll(tail, 128 - block * TAIL, 1)
            out[rows, lanes] = (grad[rows, lanes] + moved[:, :TAIL]).astype(BF16)
        return carry

    stores = []
    for step in range(STEPS):
        lax.fori_loop(step * (FIELDS // STEPS), (step + 1) * (FIELDS // STEPS), combine, 0)
        rows = pl.ds(step * (ROWS // STEPS), ROWS // STEPS)
        stores.append(pltpu.make_async_copy(out.at[rows], out_hbm.at[rows], out_sem.at[step]))
        stores[-1].start()
    for store in stores:
        store.wait()


def body(members, target, target_spectrum, legendre, wavenum):
    chunks = len(CHUNKS)
    vmem = pl.BlockSpec(memory_space=pltpu.VMEM)
    hbm = pl.BlockSpec(memory_space=pl.ANY)
    dma = pltpu.SemaphoreType.DMA
    slopes, grad, small = pl.pallas_call(
        body_kernel,
        out_shape=(
            pltpu.VMEM((ENS * OWN, 16, 128), BF16),
            pltpu.VMEM((ROWS, LON), F32),
            pltpu.VMEM((24, 128), F32),
        ),
        in_specs=[hbm, hbm, vmem, hbm, vmem, pl.BlockSpec(memory_space=pltpu.SMEM)],
        out_specs=(vmem, vmem, vmem),
        scratch_shapes=[
            pltpu.VMEM((ROWS, LON), BF16),
            pltpu.VMEM((ROWS, LON), BF16),
            pltpu.VMEM((DEV_SLOTS, LATITUDES, DEGREES), BF16),
            pltpu.VMEM((ENS * OWN, 16, 128), BF16),
            pltpu.VMEM((OWN, 16, 128), F32),
            pltpu.VMEM((ENS, OWN, 16, 128), BF16),
            pltpu.VMEM((ZS, OWN, 16, 128), BF16),
            pltpu.VMEM((ZS, OWN, 16, 128), BF16),
            pltpu.VMEM((COLS, LON), BF16),
            pltpu.VMEM((COLS, ROWS), BF16),
            pltpu.VMEM((COLS, ROWS), BF16),
            pltpu.VMEM((COLS, ROWS), BF16),
            pltpu.VMEM((COLS, ROWS), BF16),
            pltpu.VMEM((COLS, ROWS), BF16),
            pltpu.VMEM((PAIRS, COLS, 128), F32),
            pltpu.VMEM((DEV_SLOTS, FIELDS * 2 * ENS, LATITUDES), BF16),
            pltpu.VMEM((DEGREES // 128, GROUPS * 8 * ENS, 128), F32),
            pltpu.VMEM((GROUPS * 8, DEGREES), F32),
            pltpu.VMEM((GROUPS * 8, 128), F32),
            pltpu.VMEM((16, 128), F32),
            pltpu.VMEM((ENS, 16, 128), F32),
            pltpu.VMEM((ENS, 16, 128), F32),
            pltpu.VMEM((3, BAND, 128), F32),
            pltpu.VMEM((LATS, 8, 128), F32),
            pltpu.VMEM((ENS, 8, 128), F32),
            dma((chunks, ZS)), dma((chunks, ZS)),
            dma((chunks, ZS)), dma((chunks, ZS)),
            dma((chunks, ENS)), dma((chunks, ENS)),
            dma((chunks, ENS)), dma((chunks, ENS)),
            dma((PLANE,)), dma((PLANE,)),
            dma((ZS,)), dma((ZS,)),
            dma((ZS,)), dma((ZS,)),
            dma((PLANE,)), dma((PLANE,)),
            dma((ENS,)), dma((ENS,)),
            dma((LOADS,)), dma, dma, dma((chunks, 2)),
        ],
        compiler_params=pltpu.CompilerParams(
            collective_id=0, has_side_effects=True, vmem_limit_bytes=48 * 2**20
        ),
    )(
        members.reshape(ROWS, LON),
        target.reshape(ROWS, LON),
        target_spectrum,
        legendre,
        wavenum.reshape(SLOTS // 128, 128),
        wavenum,
    )
    variables = FIELDS // BATCHES
    member_grad, row_score, spec_score = pl.pallas_call(
        combine_kernel,
        out_shape=(
            jax.ShapeDtypeStruct((ROWS, LON), BF16),
            jax.ShapeDtypeStruct((BATCHES, 4, variables), F32),
            jax.ShapeDtypeStruct((BATCHES, DEV_SLOTS, variables), F32),
        ),
        in_specs=[vmem, vmem, vmem],
        out_specs=(hbm, vmem, vmem),
        scratch_shapes=[pltpu.VMEM((ROWS, LON), BF16), dma((STEPS,))],
        compiler_params=pltpu.CompilerParams(vmem_limit_bytes=16 * 2**20),
    )(slopes, grad, small)
    return (
        member_grad.reshape(members.shape),
        row_score.transpose(0, 2, 1),
        spec_score.transpose(0, 2, 1),
    )


def solution(mesh):
    in_specs = (
        P("ens", None, "var", "lat", None),
        P(None, "var", "lat", None),
        P(None, "var", ("lat", "ens"), None, None),
        P(("lat", "ens"), None, None),
        P(),
    )
    out_specs = (
        P("ens", None, "var", "lat", None),
        P(None, "var", ("lat", "ens")),
        P(None, "var", ("lat", "ens")),
    )
    return jax.shard_map(body, mesh=mesh, in_specs=in_specs, out_specs=out_specs, check_vma=False)
```

```python
import functools
import math

import jax
import jax.numpy as jnp
from jax import lax
from jax.experimental import pallas as pl
from jax.experimental.pallas import tpu as pltpu
from jax.sharding import PartitionSpec as P

LMAX = 360
MESH = pl.DeviceIdType.MESH
F32 = jnp.float32
BF16 = jnp.bfloat16
WIDTH2 = 0.0625

ENS = 16
ZS = 8
XS = 2
LATS = 8
PLANE = LATS * XS
FIELDS = 18
BATCHES = 3
BAND = 64
ROWS = FIELDS * BAND
LON = 1440
SLOTS = 384
COLS = 2 * SLOTS
DEV_SLOTS = 3
PARTS = 2 * DEV_SLOTS
LATITUDES = 512
DEGREES = 384
PAIRS = FIELDS // 2
FULL = LON // 128
TAIL = LON - FULL * 128
BLOCKS = BAND // 16
FIELD_TILES = BLOCKS * FULL + 1
TILES = FIELDS * FIELD_TILES
OWN = -(-TILES // ENS)
CHUNKS = ((0, 9), (9, 18), (27, 24))
LOADS = 6
EARLY = 4
STEPS = 6
ENTRIES = FIELDS * PARTS
GROUPS = -(-ENTRIES // 8)


def crps_block(x, y):
    offset = x - y[None]
    square = offset * offset + WIDTH2
    inverse = lax.rsqrt(square)
    near = jnp.sum(square * inverse, axis=0)
    slope = jnp.zeros_like(x)
    spread = jnp.zeros_like(y)
    half = ENS // 2
    for shift in range(1, half):
        d = x - jnp.concatenate([x[shift:], x[:shift]], axis=0)
        s = d * d + WIDTH2
        r = lax.rsqrt(s)
        spread = spread + jnp.sum(s * r, axis=0)
        ratio = d * r
        back = jnp.concatenate([ratio[ENS - shift:], ratio[: ENS - shift]], axis=0)
        slope = slope + (ratio - back)
    d = x[:half] - x[half:]
    s = d * d + WIDTH2
    r = lax.rsqrt(s)
    spread = spread + jnp.sum(s * r, axis=0)
    ratio = d * r
    slope = slope + jnp.concatenate([ratio, -ratio], axis=0)
    pair_mean = (2.0 * spread + ENS * math.sqrt(WIDTH2)) * (0.5 / (ENS * ENS))
    return near * (1.0 / ENS) - pair_mean, offset * inverse - slope * (1.0 / ENS)


def body_kernel(
    mem_hbm, tgt_hbm, tsp, leg_hbm, wave_rows, wnum,
    got_d, grad, small,
    mem, tgt, leg, tiles, own_target, got_a, stage_a, stage_d, table, send, got_b1, got_b2, got_c1, got_c2,
    wide, mixed, spectral, tspec, spec_sum, part, xs, ys, scores, score_sum, got_s,
    ax_send, ax_recv, dx_send, dx_recv, a_send, a_recv, d_send, d_recv, b1_send, b1_recv, b2_send, b2_recv,
    c1_send, c1_recv, c2_send, c2_recv, s_send, s_recv, mem_sem, tgt_sem, leg_sem, keep_sem,
):
    e = lax.axis_index("ens")
    q_me = lax.axis_index("lat")

    def ens_peer(k):
        return lax.rem(e + k, ENS)

    x_me = e // ZS
    z_me = e - x_me * ZS
    partner = (1 - x_me) * ZS + z_me
    g_me = q_me * XS + x_me

    def z_peer(k):
        odd = lax.rem(k, 2)
        away = odd * ((k + 1) // 2) + (1 - odd) * (ZS - k // 2)
        return lax.rem(z_me + away * (1 - k // ZS), ZS)

    def plane_peer(k):
        return lax.rem(g_me + k, PLANE)

    def part_of(index):
        return index + x_me * (LOADS - 1 - 2 * index)

    def mem_load(index):
        top = pl.multiple_of(part_of(index) * (ROWS // LOADS), ROWS // LOADS)
        rows = pl.ds(top, ROWS // LOADS)
        return pltpu.make_async_copy(mem_hbm.at[rows], mem.at[rows], mem_sem.at[index])

    tgt_load = pltpu.make_async_copy(tgt_hbm, tgt, tgt_sem)
    leg_load = pltpu.make_async_copy(leg_hbm, leg, leg_sem)
    for index in range(LOADS):
        mem_load(index).start()
    tgt_load.start()
    leg_load.start()
    barrier = pltpu.get_barrier_semaphore()

    def greet_ens(k, carry):
        pl.semaphore_signal(barrier, inc=1, device_id={"ens": ens_peer(k)}, device_id_type=MESH)
        return carry

    def greet_plane(k, carry):
        for x in range(XS):
            pl.semaphore_signal(
                barrier,
                inc=1,
                device_id={"ens": x * ZS + z_me, "lat": lax.rem(q_me + k, LATS)},
                device_id_type=MESH,
            )
        return carry

    lax.fori_loop(1, ENS, greet_ens, 0)
    lax.fori_loop(1, LATS, greet_plane, 0)

    def retile(field, carry):
        rows = pl.multiple_of(field * BAND, BAND)
        for block in range(BLOCKS):
            for lane in range(FULL):
                tiles[field * FIELD_TILES + block * FULL + lane] = mem[
                    pl.ds(rows + 16 * block, 16), pl.ds(lane * 128, 128)
                ]
        tails = [
            mem[pl.ds(rows + 16 * block, 16), pl.ds(FULL * 128, TAIL)].astype(F32)
            for block in range(BLOCKS)
        ]
        tiles[field * FIELD_TILES + FIELD_TILES - 1] = jnp.concatenate(tails, axis=1).astype(BF16)
        return carry

    def retile_part(index):
        mem_load(index).wait()
        first = part_of(index) * (FIELDS // LOADS)
        lax.fori_loop(first, first + FIELDS // LOADS, retile, 0)

    for index in range(EARLY):
        retile_part(index)
    tiles[pl.ds(TILES, ENS * OWN - TILES)] = jnp.zeros((ENS * OWN - TILES, 16, 128), BF16)

    def ax_copy(chunk, z):
        first, count = CHUNKS[chunk]
        return pltpu.make_async_remote_copy(
            src_ref=tiles.at[pl.ds(((1 - x_me) * ZS + z) * OWN + first, count)],
            dst_ref=stage_a.at[z, pl.ds(first, count)],
            send_sem=ax_send.at[chunk, z],
            recv_sem=ax_recv.at[chunk, z],
            device_id={"ens": partner},
            device_id_type=MESH,
        )

    def a_copy(chunk, z, slot):
        first, count = CHUNKS[chunk]
        return pltpu.make_async_remote_copy(
            src_ref=tiles.at[pl.ds((x_me * ZS + z) * OWN + first, count)],
            dst_ref=got_a.at[slot, pl.ds(first, count)],
            send_sem=a_send.at[chunk, z],
            recv_sem=a_recv.at[chunk, slot],
            device_id={"ens": x_me * ZS + z},
            device_id_type=MESH,
        )

    def a_pass(chunk, z, slot):
        first, count = CHUNKS[chunk]
        return pltpu.make_async_remote_copy(
            src_ref=stage_a.at[z, pl.ds(first, count)],
            dst_ref=got_a.at[slot, pl.ds(first, count)],
            send_sem=a_send.at[chunk, ZS + z],
            recv_sem=a_recv.at[chunk, slot],
            device_id={"ens": x_me * ZS + z},
            device_id_type=MESH,
        )

    def ax_start(chunk):
        def step(k, carry):
            ax_copy(chunk, z_peer(k)).start()
            return carry

        lax.fori_loop(1, ZS + 1, step, 0)

    def a_start(chunk):
        def step(k, carry):
            a_copy(chunk, z_peer(k), e).start()
            return carry

        lax.fori_loop(1, ZS, step, 0)
        first, count = CHUNKS[chunk]
        got_a[e, pl.ds(first, count)] = tiles[pl.ds(e * OWN + first, count)]

    def a_forward(chunk):
        def step(k, carry):
            ax_copy(chunk, z_peer(k)).wait_recv()
            a_pass(chunk, z_peer(k), partner).start()
            return carry

        lax.fori_loop(1, ZS, step, 0)
        ax_copy(chunk, z_me).wait_recv()
        first, count = CHUNKS[chunk]
        got_a[partner, pl.ds(first, count)] = stage_a[z_me, pl.ds(first, count)]

    def a_wait(chunk):
        def step(k, carry):
            a_copy(chunk, z_me, x_me * ZS + z_peer(k)).wait_recv()
            a_pass(chunk, z_me, (1 - x_me) * ZS + z_peer(k)).wait_recv()
            return carry

        lax.fori_loop(1, ZS, step, 0)

    def a_done(chunk):
        def step(k, carry):
            a_copy(chunk, z_peer(k), e).wait_send()
            a_pass(chunk, z_peer(k), partner).wait_send()
            return carry

        def step_x(z, carry):
            ax_copy(chunk, z).wait_send()
            return carry

        lax.fori_loop(1, ZS, step, 0)
        lax.fori_loop(0, ZS, step_x, 0)

    pl.semaphore_wait(barrier, ENS - 1 + XS * (LATS - 1))
    for chunk in range(len(CHUNKS)):
        a_start(chunk)
    for index in range(EARLY, LOADS):
        retile_part(index)
    ax_start(0)

    def table_rows(index, carry):
        rows = pl.ds(pl.multiple_of(index * 64, 64), 64)
        lane = lax.broadcasted_iota(jnp.int32, (64, 128), 1).astype(F32)
        row = lax.broadcasted_iota(jnp.int32, (64, 128), 0)
        group = wave_rows[pl.ds(index // 4, 1), :].astype(F32)
        at = lax.rem(index, 4) * 32 + row // 2
        wave = jnp.sum(
            jnp.where(lax.broadcasted_iota(jnp.int32, (64, 128), 1) == at, group, 0.0),
            axis=1,
            keepdims=True,
        )

        def angles(turns):
            turns = turns - LON * jnp.floor(turns * (1.0 / LON))
            return turns * (2.0 * math.pi / LON)

        fine = angles(wave * lane)
        coarse = angles(wave * (128.0 * jnp.minimum(lane, 15.0)))
        cos_b, sin_b = jnp.cos(fine), jnp.sin(fine)
        factor = 1.0 / math.sqrt(LON)
        cos_a, sin_a = jnp.cos(coarse) * factor, jnp.sin(coarse) * factor
        real = lax.rem(row, 2) == 0
        first = jnp.where(real, cos_a, -sin_a)
        second = jnp.where(real, -sin_a, -cos_a)
        for lane_block in range(FULL + 1):
            width = min(128, LON - lane_block * 128)
            value = first[:, lane_block : lane_block + 1] * cos_b
            value = value + second[:, lane_block : lane_block + 1] * sin_b
            table[rows, pl.ds(lane_block * 128, width)] = value[:, :width].astype(BF16)
        return carry

    lax.fori_loop(0, COLS // 64, table_rows, 0)

    def forward(index, carry):
        lanes = pl.ds(pl.multiple_of(index * 384, 384), 384)
        value = lax.dot_general(
            table[...], mem[lanes, :], (((1,), (1,)), ((), ())), preferred_element_type=F32
        )
        send[:, lanes] = value.astype(BF16)
        return carry

    lax.fori_loop(0, ROWS // 384, forward, 0)

    per_plane = COLS // PLANE
    per_z = COLS // ZS

    def plane_copy(source, got, s_sem, r_sem, peer, slot):
        return pltpu.make_async_remote_copy(
            src_ref=source.at[pl.ds(peer * per_plane, per_plane)],
            dst_ref=got.at[pl.ds(slot * per_plane, per_plane)],
            send_sem=s_sem.at[peer],
            recv_sem=r_sem.at[slot],
            device_id={"ens": lax.rem(peer, XS) * ZS + z_me, "lat": peer // XS},
            device_id_type=MESH,
        )

    def z_copy(source, got, s_sem, r_sem, peer, slot):
        return pltpu.make_async_remote_copy(
            src_ref=source.at[pl.ds(peer * per_z, per_z)],
            dst_ref=got.at[pl.ds(slot * per_z, per_z)],
            send_sem=s_sem.at[peer],
            recv_sem=r_sem.at[slot],
            device_id={"ens": x_me * ZS + peer},
            device_id_type=MESH,
        )

    def exchange(copy, count, peer_of, me, size, got, s_sem, r_sem):
        def start(k, carry):
            copy(send, got, s_sem, r_sem, peer_of(k), me).start()
            return carry

        lax.fori_loop(1, count, start, 0)
        mine = pl.ds(pl.multiple_of(me * size, size), size)
        got[mine, :] = send[mine, :]

    def finish_near(copy, count, peer_of, me, got, s_sem, r_sem):
        for k in (1, 2, 3, 4):
            copy(send, got, s_sem, r_sem, me, peer_of(k)).wait_recv()

    def finish_far(copy, count, peer_of, me, got, s_sem, r_sem):
        for k in range(5, count):
            copy(send, got, s_sem, r_sem, me, peer_of(k)).wait_recv()
        for k in range(1, count):
            copy(send, got, s_sem, r_sem, peer_of(k), me).wait_send()

    def finish(copy, count, peer_of, me, got, s_sem, r_sem):
        def wait(k, carry):
            copy(send, got, s_sem, r_sem, peer_of(k), me).wait_send()
            copy(send, got, s_sem, r_sem, me, peer_of(k)).wait_recv()
            return carry

        lax.fori_loop(1, count, wait, 0)

    def widen(got):
        def step(index, carry):
            rows = pl.ds(pl.multiple_of(index * 48, 48), 48)
            for pair in range(PAIRS):
                wide[pair, rows, :] = got[rows, pl.ds(pair * 128, 128)].astype(F32)
            return carry

        lax.fori_loop(0, COLS // 48, step, 0)

    exchange(plane_copy, PLANE, plane_peer, g_me, per_plane, got_b1, b1_send, b1_recv)

    tgt_load.wait()

    def target_tile(index, carry):
        tile = e * OWN + index
        field = tile // FIELD_TILES
        place = tile - field * FIELD_TILES

        @pl.when(jnp.logical_and(place < FIELD_TILES - 1, tile < TILES))
        def _():
            block = place // FULL
            lane = place - block * FULL
            rows = pl.multiple_of(field * BAND + block * 16, 16)
            own_target[index] = tgt[
                pl.ds(rows, 16), pl.ds(pl.multiple_of(lane * 128, 128), 128)
            ].astype(F32)

        @pl.when(jnp.logical_and(place == FIELD_TILES - 1, tile < TILES))
        def _():
            rows = pl.multiple_of(field * BAND, BAND)
            tails = [
                tgt[pl.ds(rows + 16 * block, 16), pl.ds(FULL * 128, TAIL)].astype(F32)
                for block in range(BLOCKS)
            ]
            own_target[index] = jnp.concatenate(tails, axis=1)

        @pl.when(tile >= TILES)
        def _():
            own_target[index] = jnp.zeros((16, 128), F32)

        return carry

    lax.fori_loop(0, OWN, target_tile, 0)
    field_first = (e * OWN) // FIELD_TILES
    scores[...] = jnp.zeros_like(scores)
    for b in range(BATCHES):
        for v in range(FIELDS // BATCHES):
            for s in range(DEV_SLOTS):
                row = (b * (FIELDS // BATCHES) + v) * PARTS + 2 * s
                tspec[pl.ds(row, 2), :] = tsp[b, v, s].astype(F32)
    tspec[pl.ds(ENTRIES, GROUPS * 8 - ENTRIES), :] = jnp.zeros((GROUPS * 8 - ENTRIES, DEGREES), F32)
    spec_sum[...] = jnp.zeros_like(spec_sum)

    a_forward(0)
    finish(plane_copy, PLANE, plane_peer, g_me, got_b1, b1_send, b1_recv)
    widen(got_b1)

    def regroup_b(peer, carry):
        for pair in range(PAIRS):
            for piece in range(PARTS):
                value = wide[pair, pl.ds(peer * PARTS + piece, PLANE, stride=per_plane), :]
                rows = pl.multiple_of(peer * per_z + PLANE * piece, PLANE)
                send[pl.ds(rows, PLANE), pl.ds(pair * 128, 128)] = value.astype(BF16)
        return carry

    lax.fori_loop(0, ZS, regroup_b, 0)
    exchange(z_copy, ZS, z_peer, z_me, per_z, got_b2, b2_send, b2_recv)
    ax_start(1)
    ax_start(2)

    def grid_tile(index, carry):
        def load(member, inner):
            xs[member] = got_a[member, index].astype(F32)
            return inner

        lax.fori_loop(0, ENS, load, 0, unroll=True)
        for top in (0, 8):
            rows = pl.ds(top, 8)
            score, slope = crps_block(xs[:, rows, :], own_target[index, rows, :])
            ys[:, rows, :] = slope
            part[rows, :] = score

        def store(member, inner):
            got_a[member, index] = ys[member].astype(BF16)
            return inner

        lax.fori_loop(0, ENS, store, 0, unroll=True)
        tile = e * OWN + index
        field = tile // FIELD_TILES
        place = tile - field * FIELD_TILES
        local = field - field_first

        @pl.when(place < FIELD_TILES - 1)
        def _():
            rows = pl.ds(pl.multiple_of(place // FULL * 16, 16), 16)
            scores[local, rows, :] = scores[local, rows, :] + part[...]

        @pl.when(place == FIELD_TILES - 1)
        def _():
            segment = lax.broadcasted_iota(jnp.int32, (16, 128), 1) // TAIL
            for block in range(BLOCKS):
                rows = pl.ds(16 * block, 16)
                scores[local, rows, :] = scores[local, rows, :] + jnp.where(
                    segment == block, part[...], 0.0
                )

        return carry

    def dx_copy(chunk, z):
        first, count = CHUNKS[chunk]
        return pltpu.make_async_remote_copy(
            src_ref=got_a.at[(1 - x_me) * ZS + z, pl.ds(first, count)],
            dst_ref=stage_d.at[z, pl.ds(first, count)],
            send_sem=dx_send.at[chunk, z],
            recv_sem=dx_recv.at[chunk, z],
            device_id={"ens": partner},
            device_id_type=MESH,
        )

    def d_copy(chunk, z, slot):
        first, count = CHUNKS[chunk]
        return pltpu.make_async_remote_copy(
            src_ref=got_a.at[x_me * ZS + z, pl.ds(first, count)],
            dst_ref=got_d.at[pl.ds(slot * OWN + first, count)],
            send_sem=d_send.at[chunk, z],
            recv_sem=d_recv.at[chunk, slot],
            device_id={"ens": x_me * ZS + z},
            device_id_type=MESH,
        )

    def d_pass(chunk, z, slot):
        first, count = CHUNKS[chunk]
        return pltpu.make_async_remote_copy(
            src_ref=stage_d.at[z, pl.ds(first, count)],
            dst_ref=got_d.at[pl.ds(slot * OWN + first, count)],
            send_sem=d_send.at[chunk, ZS + z],
            recv_sem=d_recv.at[chunk, slot],
            device_id={"ens": x_me * ZS + z},
            device_id_type=MESH,
        )

    def d_keep(chunk):
        first, count = CHUNKS[chunk]
        return pltpu.make_async_copy(
            got_a.at[e, pl.ds(first, count)],
            got_d.at[pl.ds(e * OWN + first, count)],
            keep_sem.at[chunk, 0],
        )

    def d_cross(chunk):
        first, count = CHUNKS[chunk]
        return pltpu.make_async_copy(
            stage_d.at[z_me, pl.ds(first, count)],
            got_d.at[pl.ds(partner * OWN + first, count)],
            keep_sem.at[chunk, 1],
        )

    def dx_start(chunk):
        def step(k, carry):
            dx_copy(chunk, z_peer(k)).start()
            return carry

        lax.fori_loop(1, ZS + 1, step, 0)

    def d_start(chunk):
        def step(k, carry):
            d_copy(chunk, z_peer(k), e).start()
            return carry

        lax.fori_loop(1, ZS, step, 0)
        d_keep(chunk).start()

    def d_forward(chunk):
        def step(k, carry):
            dx_copy(chunk, z_peer(k)).wait_recv()
            d_pass(chunk, z_peer(k), partner).start()
            return carry

        lax.fori_loop(1, ZS, step, 0)
        dx_copy(chunk, z_me).wait_recv()
        d_cross(chunk).start()

    def d_wait(chunk):
        def step(k, carry):
            d_copy(chunk, z_peer(k), e).wait_send()
            d_pass(chunk, z_peer(k), partner).wait_send()
            d_copy(chunk, z_me, x_me * ZS + z_peer(k)).wait_recv()
            d_pass(chunk, z_me, (1 - x_me) * ZS + z_peer(k)).wait_recv()
            return carry

        def step_x(z, carry):
            dx_copy(chunk, z).wait_send()
            return carry

        lax.fori_loop(1, ZS, step, 0)
        lax.fori_loop(0, ZS, step_x, 0)
        d_keep(chunk).wait()
        d_cross(chunk).wait()

    def grid_chunk(chunk):
        a_wait(chunk)
        first, count = CHUNKS[chunk]
        lax.fori_loop(first, first + count, grid_tile, 0)

    grid_chunk(0)
    dx_start(0)

    finish_near(z_copy, ZS, z_peer, z_me, got_b2, b2_send, b2_recv)
    a_forward(1)
    finish_far(z_copy, ZS, z_peer, z_me, got_b2, b2_send, b2_recv)
    a_forward(2)
    widen(got_b2)
    low = lax.broadcasted_iota(jnp.int32, (16, 128), 1) < 64

    def swap(even, odd):
        first = jnp.where(low, even, pltpu.roll(odd, 64, 1))
        second = jnp.where(low, pltpu.roll(even, 64, 1), odd)
        return first, second

    half_rows = 2 * PAIRS * ENS

    def legendre_in(index, carry):
        pair = index // PARTS
        piece = index - pair * PARTS
        slot = piece // 2
        c = piece - 2 * slot
        row = pl.multiple_of((c * PAIRS + pair) * ENS, ENS)
        for twin in range(LATS // 2):
            start = piece * PLANE + 2 * XS * twin
            rows = [wide[pair, pl.ds(start + i, ZS, stride=per_z), :] for i in range(2 * XS)]
            even = jnp.concatenate(rows[:XS], axis=0)
            odd = jnp.concatenate(rows[XS:], axis=0)
            first, second = swap(even, odd)
            mixed[slot, pl.ds(row, ENS), pl.ds(twin * 128, 128)] = first.astype(BF16)
            mixed[slot, pl.ds(row + half_rows, ENS), pl.ds(twin * 128, 128)] = second.astype(BF16)
        return carry

    lax.fori_loop(0, PAIRS * PARTS, legendre_in, 0)
    for lane_block in range(DEGREES // 128):
        spectral[lane_block, pl.ds(ENTRIES * ENS, GROUPS * 8 * ENS - ENTRIES * ENS), :] = jnp.zeros(
            (GROUPS * 8 * ENS - ENTRIES * ENS, 128), F32
        )

    leg_load.wait()

    def analysis(slot, carry):
        value = jnp.dot(mixed[slot], leg[slot], preferred_element_type=F32)
        for field in range(FIELDS):
            for c in range(2):
                row = (field % 2) * half_rows + (c * PAIRS + field // 2) * ENS
                to = pl.multiple_of((field * PARTS + 2 * slot + c) * ENS, ENS)
                for lane_block in range(DEGREES // 128):
                    spectral[lane_block, pl.ds(to, ENS), :] = value[
                        row : row + ENS, lane_block * 128 : lane_block * 128 + 128
                    ]
        return carry

    lax.fori_loop(0, DEV_SLOTS, analysis, 0)

    first_slot = (q_me * ENS + e) * DEV_SLOTS
    slot_waves = [wnum[first_slot + s] for s in range(DEV_SLOTS)]

    def spectral_group(index, carry):
        group = index // (DEGREES // 128)
        lane_block = index - group * (DEGREES // 128)
        entry = group * 8 + lax.broadcasted_iota(jnp.int32, (8, 128), 0)
        slot = lax.rem(entry // 2, DEV_SLOTS)
        wave = jnp.where(slot == 0, slot_waves[0], jnp.where(slot == 1, slot_waves[1], slot_waves[2]))
        degree = lane_block * 128 + lax.broadcasted_iota(jnp.int32, (8, 128), 1)
        usable = jnp.logical_and(degree >= wave, degree <= LMAX)
        weight = jnp.where(usable, jnp.where(wave == 0, 1.0, 2.0), 0.0)
        base = group * (8 * ENS)
        x = jnp.stack(
            [spectral[lane_block, pl.ds(base + m, 8, stride=ENS), :] for m in range(ENS)], axis=0
        )
        x = jnp.where(usable[None], x, 0.0).astype(BF16).astype(F32)
        rows = pl.ds(pl.multiple_of(group * 8, 8), 8)
        y = tspec[rows, pl.ds(pl.multiple_of(lane_block * 128, 128), 128)]
        score, slope = crps_block(x, y)
        spec_sum[rows, :] = spec_sum[rows, :] + score * weight
        slope = slope * weight[None]
        for m in range(ENS):
            spectral[lane_block, pl.ds(base + m, 8, stride=ENS), :] = slope[m]
        return carry

    lax.fori_loop(0, GROUPS * (DEGREES // 128), spectral_group, 0)

    def synthesis(slot, carry):
        for field in range(FIELDS):
            for c in range(2):
                row = (field % 2) * half_rows + (c * PAIRS + field // 2) * ENS
                at = pl.multiple_of((field * PARTS + 2 * slot + c) * ENS, ENS)
                for lane_block in range(DEGREES // 128):
                    mixed[slot, pl.ds(row, ENS), pl.ds(lane_block * 128, 128)] = spectral[
                        lane_block, pl.ds(at, ENS), :
                    ].astype(BF16)
        value = lax.dot_general(
            mixed[slot, :, pl.ds(0, DEGREES)], leg[slot], (((1,), (1,)), ((), ())),
            preferred_element_type=F32,
        )
        for pair in range(PAIRS):
            for c in range(2):
                row = (c * PAIRS + pair) * ENS
                for twin in range(LATS // 2):
                    lanes = slice(twin * 128, twin * 128 + 128)
                    even, odd = swap(
                        value[row : row + ENS, lanes],
                        value[row + half_rows : row + half_rows + ENS, lanes],
                    )
                    start = (2 * slot + c) * PLANE + 2 * XS * twin
                    for i in range(XS):
                        members = slice(i * ZS, i * ZS + ZS)
                        wide[pair, pl.ds(start + i, ZS, stride=per_z), :] = even[members]
                        wide[pair, pl.ds(start + XS + i, ZS, stride=per_z), :] = odd[members]
        return carry

    lax.fori_loop(0, DEV_SLOTS, synthesis, 0)

    def narrow(index, carry):
        rows = pl.ds(pl.multiple_of(index * 48, 48), 48)
        for pair in range(PAIRS):
            send[rows, pl.ds(pair * 128, 128)] = wide[pair, rows, :].astype(BF16)
        return carry

    lax.fori_loop(0, COLS // 48, narrow, 0)
    exchange(z_copy, ZS, z_peer, z_me, per_z, got_c1, c1_send, c1_recv)
    grid_chunk(1)
    dx_start(1)
    grid_chunk(2)
    dx_start(2)
    finish_near(z_copy, ZS, z_peer, z_me, got_c1, c1_send, c1_recv)
    d_start(0)
    d_forward(0)

    lane = lax.broadcasted_iota(jnp.int32, (BAND, 128), 1)
    total = jnp.zeros((BAND, 128), F32)
    for local in range(3):
        rows_sum = jnp.sum(scores[local], axis=1, keepdims=True) * (1.0 / LON)
        total = total + jnp.where(lane == field_first + local, rows_sum, 0.0)
    turn = lax.rem(lax.broadcasted_iota(jnp.int32, (BAND, 128), 0), 4)
    packed = total
    for place in range(1, 4):
        packed = jnp.where(turn == place, pltpu.roll(total, 32 * place, 1), packed)
    for peer in range(ENS):
        score_sum[peer] = jnp.sum(packed[4 * peer : 4 * peer + 4], axis=0, keepdims=True)

    def s_copy(peer, slot):
        return pltpu.make_async_remote_copy(
            src_ref=score_sum.at[peer],
            dst_ref=got_s.at[slot],
            send_sem=s_send.at[peer],
            recv_sem=s_recv.at[slot],
            device_id={"ens": peer},
            device_id_type=MESH,
        )

    def s_start(k, carry):
        s_copy(ens_peer(k), e).start()
        return carry

    lax.fori_loop(1, ENS, s_start, 0)
    got_s[e] = score_sum[e]

    finish_far(z_copy, ZS, z_peer, z_me, got_c1, c1_send, c1_recv)
    d_start(1)
    d_forward(1)
    d_start(2)
    d_forward(2)
    widen(got_c1)

    def regroup_c(place, carry):
        rows = pl.ds(pl.multiple_of(place * per_plane, per_plane), per_plane)
        for pair in range(PAIRS):
            send[rows, pl.ds(pair * 128, 128)] = wide[
                pair, pl.ds(place, per_plane, stride=PLANE), :
            ].astype(BF16)
        return carry

    lax.fori_loop(0, PLANE, regroup_c, 0)
    exchange(plane_copy, PLANE, plane_peer, g_me, per_plane, got_c2, c2_send, c2_recv)
    sums = jnp.sum(spec_sum[...], axis=1, keepdims=True) * (1.0 / (2.0 * (LMAX + 1)))
    entry = lax.broadcasted_iota(jnp.int32, (GROUPS * 8, 128), 0)
    variables = FIELDS // BATCHES
    place = lax.broadcasted_iota(jnp.int32, (GROUPS * 8, 128), 1)
    sums = jnp.where(place == lax.rem(entry // PARTS, variables), sums, 0.0)
    for b in range(BATCHES):
        for slot in range(DEV_SLOTS):
            chosen = jnp.logical_and(
                entry // (PARTS * variables) == b, lax.rem(entry, PARTS) // 2 == slot
            )
            small[pl.ds(8 + b * DEV_SLOTS + slot, 1), :] = jnp.sum(
                jnp.where(chosen, sums, 0.0), axis=0, keepdims=True
            )
    finish(plane_copy, PLANE, plane_peer, g_me, got_c2, c2_send, c2_recv)

    def backward(index, carry):
        lanes = pl.ds(pl.multiple_of(index * 384, 384), 384)
        grad[lanes, :] = lax.dot_general(
            got_c2[:, lanes], table[...], (((0,), (0,)), ((), ())), preferred_element_type=F32
        )
        return carry

    lax.fori_loop(0, ROWS // 384, backward, 0)

    def s_wait(k, carry):
        s_copy(ens_peer(k), e).wait_send()
        s_copy(e, ens_peer(k)).wait_recv()
        return carry

    for chunk in range(len(CHUNKS)):
        a_done(chunk)
    for chunk in range(len(CHUNKS)):
        d_wait(chunk)
    lax.fori_loop(1, ENS, s_wait, 0)
    small[pl.ds(0, 1), :] = jnp.sum(got_s[...], axis=0)


def combine_kernel(got_d, grad, small, out_hbm, row_out, spec_out, out, out_sem):
    variables = FIELDS // BATCHES
    for b in range(BATCHES):
        for row in range(4):
            lanes = pl.ds(32 * row + b * variables, variables)
            row_out[b, pl.ds(row, 1), :] = small[pl.ds(0, 1), lanes]
        spec_out[b] = small[pl.ds(8 + b * DEV_SLOTS, DEV_SLOTS), pl.ds(0, variables)]

    def combine(field, carry):
        top = pl.multiple_of(field * BAND, BAND)
        tail = got_d[field * FIELD_TILES + FIELD_TILES - 1].astype(F32)
        for block in range(BLOCKS):
            rows = pl.ds(top + 16 * block, 16)
            for lane_block in range(FULL):
                lanes = pl.ds(lane_block * 128, 128)
                slope = got_d[field * FIELD_TILES + block * FULL + lane_block].astype(F32)
                out[rows, lanes] = (grad[rows, lanes] + slope).astype(BF16)
            lanes = pl.ds(FULL * 128, TAIL)
            moved = tail if block == 0 else pltpu.roll(tail, 128 - block * TAIL, 1)
            out[rows, lanes] = (grad[rows, lanes] + moved[:, :TAIL]).astype(BF16)
        return carry

    stores = []
    for step in range(STEPS):
        lax.fori_loop(step * (FIELDS // STEPS), (step + 1) * (FIELDS // STEPS), combine, 0)
        rows = pl.ds(step * (ROWS // STEPS), ROWS // STEPS)
        stores.append(pltpu.make_async_copy(out.at[rows], out_hbm.at[rows], out_sem.at[step]))
        stores[-1].start()
    for store in stores:
        store.wait()


def body(members, target, target_spectrum, legendre, wavenum):
    chunks = len(CHUNKS)
    vmem = pl.BlockSpec(memory_space=pltpu.VMEM)
    hbm = pl.BlockSpec(memory_space=pl.ANY)
    dma = pltpu.SemaphoreType.DMA
    slopes, grad, small = pl.pallas_call(
        body_kernel,
        out_shape=(
            pltpu.VMEM((ENS * OWN, 16, 128), BF16),
            pltpu.VMEM((ROWS, LON), F32),
            pltpu.VMEM((24, 128), F32),
        ),
        in_specs=[hbm, hbm, vmem, hbm, vmem, pl.BlockSpec(memory_space=pltpu.SMEM)],
        out_specs=(vmem, vmem, vmem),
        scratch_shapes=[
            pltpu.VMEM((ROWS, LON), BF16),
            pltpu.VMEM((ROWS, LON), BF16),
            pltpu.VMEM((DEV_SLOTS, LATITUDES, DEGREES), BF16),
            pltpu.VMEM((ENS * OWN, 16, 128), BF16),
            pltpu.VMEM((OWN, 16, 128), F32),
            pltpu.VMEM((ENS, OWN, 16, 128), BF16),
            pltpu.VMEM((ZS, OWN, 16, 128), BF16),
            pltpu.VMEM((ZS, OWN, 16, 128), BF16),
            pltpu.VMEM((COLS, LON), BF16),
            pltpu.VMEM((COLS, ROWS), BF16),
            pltpu.VMEM((COLS, ROWS), BF16),
            pltpu.VMEM((COLS, ROWS), BF16),
            pltpu.VMEM((COLS, ROWS), BF16),
            pltpu.VMEM((COLS, ROWS), BF16),
            pltpu.VMEM((PAIRS, COLS, 128), F32),
            pltpu.VMEM((DEV_SLOTS, FIELDS * 2 * ENS, LATITUDES), BF16),
            pltpu.VMEM((DEGREES // 128, GROUPS * 8 * ENS, 128), F32),
            pltpu.VMEM((GROUPS * 8, DEGREES), F32),
            pltpu.VMEM((GROUPS * 8, 128), F32),
            pltpu.VMEM((16, 128), F32),
            pltpu.VMEM((ENS, 16, 128), F32),
            pltpu.VMEM((ENS, 16, 128), F32),
            pltpu.VMEM((3, BAND, 128), F32),
            pltpu.VMEM((ENS, 1, 128), F32),
            pltpu.VMEM((ENS, 1, 128), F32),
            dma((chunks, ZS)), dma((chunks, ZS)),
            dma((chunks, ZS)), dma((chunks, ZS)),
            dma((chunks, ENS)), dma((chunks, ENS)),
            dma((chunks, ENS)), dma((chunks, ENS)),
            dma((PLANE,)), dma((PLANE,)),
            dma((ZS,)), dma((ZS,)),
            dma((ZS,)), dma((ZS,)),
            dma((PLANE,)), dma((PLANE,)),
            dma((ENS,)), dma((ENS,)),
            dma((LOADS,)), dma, dma, dma((chunks, 2)),
        ],
        compiler_params=pltpu.CompilerParams(
            collective_id=0, has_side_effects=True, vmem_limit_bytes=48 * 2**20
        ),
    )(
        members.reshape(ROWS, LON),
        target.reshape(ROWS, LON),
        target_spectrum,
        legendre,
        wavenum.reshape(SLOTS // 128, 128),
        wavenum,
    )
    variables = FIELDS // BATCHES
    member_grad, row_score, spec_score = pl.pallas_call(
        combine_kernel,
        out_shape=(
            jax.ShapeDtypeStruct((ROWS, LON), BF16),
            jax.ShapeDtypeStruct((BATCHES, 4, variables), F32),
            jax.ShapeDtypeStruct((BATCHES, DEV_SLOTS, variables), F32),
        ),
        in_specs=[vmem, vmem, vmem],
        out_specs=(hbm, vmem, vmem),
        scratch_shapes=[pltpu.VMEM((ROWS, LON), BF16), dma((STEPS,))],
        compiler_params=pltpu.CompilerParams(vmem_limit_bytes=16 * 2**20),
    )(slopes, grad, small)
    return (
        member_grad.reshape(members.shape),
        row_score.transpose(0, 2, 1),
        spec_score.transpose(0, 2, 1),
    )


def solution(mesh):
    in_specs = (
        P("ens", None, "var", "lat", None),
        P(None, "var", "lat", None),
        P(None, "var", ("lat", "ens"), None, None),
        P(("lat", "ens"), None, None),
        P(),
    )
    out_specs = (
        P("ens", None, "var", "lat", None),
        P(None, "var", ("lat", "ens")),
        P(None, "var", ("lat", "ens")),
    )
    return jax.shard_map(body, mesh=mesh, in_specs=in_specs, out_specs=out_specs, check_vma=False)
```

```python
import functools
import math

import jax
import jax.numpy as jnp
from jax import lax
from jax.experimental import pallas as pl
from jax.experimental.pallas import tpu as pltpu
from jax.sharding import PartitionSpec as P

LMAX = 360
MESH = pl.DeviceIdType.MESH
F32 = jnp.float32
BF16 = jnp.bfloat16
WIDTH2 = 0.0625

ENS = 16
ZS = 8
XS = 2
LATS = 8
PLANE = LATS * XS
FIELDS = 18
BATCHES = 3
BAND = 64
ROWS = FIELDS * BAND
LON = 1440
SLOTS = 384
COLS = 2 * SLOTS
DEV_SLOTS = 3
PARTS = 2 * DEV_SLOTS
LATITUDES = 512
DEGREES = 384
PAIRS = FIELDS // 2
FULL = LON // 128
TAIL = LON - FULL * 128
BLOCKS = BAND // 16
FIELD_TILES = BLOCKS * FULL + 1
TILES = FIELDS * FIELD_TILES
OWN = -(-TILES // ENS)
CHUNKS = ((0, 9), (9, 18), (27, 24))
LOADS = 6
EARLY = 4
STEPS = 18
ENTRIES = FIELDS * PARTS
GROUPS = -(-ENTRIES // 8)


def crps_block(x, y):
    offset = x - y[None]
    square = offset * offset + WIDTH2
    inverse = lax.rsqrt(square)
    near = jnp.sum(square * inverse, axis=0)
    slope = jnp.zeros_like(x)
    spread = jnp.zeros_like(y)
    half = ENS // 2
    for shift in range(1, half):
        d = x - jnp.concatenate([x[shift:], x[:shift]], axis=0)
        s = d * d + WIDTH2
        r = lax.rsqrt(s)
        spread = spread + jnp.sum(s * r, axis=0)
        ratio = d * r
        back = jnp.concatenate([ratio[ENS - shift:], ratio[: ENS - shift]], axis=0)
        slope = slope + (ratio - back)
    d = x[:half] - x[half:]
    s = d * d + WIDTH2
    r = lax.rsqrt(s)
    spread = spread + jnp.sum(s * r, axis=0)
    ratio = d * r
    slope = slope + jnp.concatenate([ratio, -ratio], axis=0)
    pair_mean = (2.0 * spread + ENS * math.sqrt(WIDTH2)) * (0.5 / (ENS * ENS))
    return near * (1.0 / ENS) - pair_mean, offset * inverse - slope * (1.0 / ENS)


def body_kernel(
    mem_hbm, tgt_hbm, tsp, leg_hbm, wave_rows, wnum,
    got_d, grad, small,
    mem, tgt, leg, tiles, own_target, got_a, stage_a, stage_d, table, send, got_b1, got_b2, got_c1, got_c2,
    wide, mixed, spectral, tspec, spec_sum, part, xs, ys, scores, score_sum, got_s,
    ax_send, ax_recv, dx_send, dx_recv, a_send, a_recv, d_send, d_recv, b1_send, b1_recv, b2_send, b2_recv,
    c1_send, c1_recv, c2_send, c2_recv, s_send, s_recv, mem_sem, tgt_sem, leg_sem, keep_sem,
):
    e = lax.axis_index("ens")
    q_me = lax.axis_index("lat")

    def ens_peer(k):
        return lax.rem(e + k, ENS)

    x_me = e // ZS
    z_me = e - x_me * ZS
    partner = (1 - x_me) * ZS + z_me
    g_me = q_me * XS + x_me

    def z_peer(k):
        odd = lax.rem(k, 2)
        away = odd * ((k + 1) // 2) + (1 - odd) * (ZS - k // 2)
        return lax.rem(z_me + away * (1 - k // ZS), ZS)

    def plane_peer(k):
        return lax.rem(g_me + k, PLANE)

    def part_of(index):
        return index + x_me * (LOADS - 1 - 2 * index)

    def mem_load(index):
        top = pl.multiple_of(part_of(index) * (ROWS // LOADS), ROWS // LOADS)
        rows = pl.ds(top, ROWS // LOADS)
        return pltpu.make_async_copy(mem_hbm.at[rows], mem.at[rows], mem_sem.at[index])

    tgt_load = pltpu.make_async_copy(tgt_hbm, tgt, tgt_sem)
    leg_load = pltpu.make_async_copy(leg_hbm, leg, leg_sem)
    for index in range(LOADS):
        mem_load(index).start()
    tgt_load.start()
    leg_load.start()
    barrier = pltpu.get_barrier_semaphore()

    def greet_ens(k, carry):
        pl.semaphore_signal(barrier, inc=1, device_id={"ens": ens_peer(k)}, device_id_type=MESH)
        return carry

    def greet_plane(k, carry):
        for x in range(XS):
            pl.semaphore_signal(
                barrier,
                inc=1,
                device_id={"ens": x * ZS + z_me, "lat": lax.rem(q_me + k, LATS)},
                device_id_type=MESH,
            )
        return carry

    lax.fori_loop(1, ENS, greet_ens, 0)
    lax.fori_loop(1, LATS, greet_plane, 0)

    def retile(field, carry):
        rows = pl.multiple_of(field * BAND, BAND)
        for block in range(BLOCKS):
            for lane in range(FULL):
                tiles[field * FIELD_TILES + block * FULL + lane] = mem[
                    pl.ds(rows + 16 * block, 16), pl.ds(lane * 128, 128)
                ]
        tails = [
            mem[pl.ds(rows + 16 * block, 16), pl.ds(FULL * 128, TAIL)].astype(F32)
            for block in range(BLOCKS)
        ]
        tiles[field * FIELD_TILES + FIELD_TILES - 1] = jnp.concatenate(tails, axis=1).astype(BF16)
        return carry

    def retile_part(index):
        mem_load(index).wait()
        first = part_of(index) * (FIELDS // LOADS)
        lax.fori_loop(first, first + FIELDS // LOADS, retile, 0)

    for index in range(EARLY):
        retile_part(index)
    tiles[pl.ds(TILES, ENS * OWN - TILES)] = jnp.zeros((ENS * OWN - TILES, 16, 128), BF16)

    def ax_copy(chunk, z):
        first, count = CHUNKS[chunk]
        return pltpu.make_async_remote_copy(
            src_ref=tiles.at[pl.ds(((1 - x_me) * ZS + z) * OWN + first, count)],
            dst_ref=stage_a.at[z, pl.ds(first, count)],
            send_sem=ax_send.at[chunk, z],
            recv_sem=ax_recv.at[chunk, z],
            device_id={"ens": partner},
            device_id_type=MESH,
        )

    def a_copy(chunk, z, slot):
        first, count = CHUNKS[chunk]
        return pltpu.make_async_remote_copy(
            src_ref=tiles.at[pl.ds((x_me * ZS + z) * OWN + first, count)],
            dst_ref=got_a.at[slot, pl.ds(first, count)],
            send_sem=a_send.at[chunk, z],
            recv_sem=a_recv.at[chunk, slot],
            device_id={"ens": x_me * ZS + z},
            device_id_type=MESH,
        )

    def a_pass(chunk, z, slot):
        first, count = CHUNKS[chunk]
        return pltpu.make_async_remote_copy(
            src_ref=stage_a.at[z, pl.ds(first, count)],
            dst_ref=got_a.at[slot, pl.ds(first, count)],
            send_sem=a_send.at[chunk, ZS + z],
            recv_sem=a_recv.at[chunk, slot],
            device_id={"ens": x_me * ZS + z},
            device_id_type=MESH,
        )

    def ax_start(chunk):
        def step(k, carry):
            ax_copy(chunk, z_peer(k)).start()
            return carry

        lax.fori_loop(1, ZS + 1, step, 0)

    def a_start(chunk):
        def step(k, carry):
            a_copy(chunk, z_peer(k), e).start()
            return carry

        lax.fori_loop(1, ZS, step, 0)
        first, count = CHUNKS[chunk]
        got_a[e, pl.ds(first, count)] = tiles[pl.ds(e * OWN + first, count)]

    def a_forward(chunk):
        def step(k, carry):
            ax_copy(chunk, z_peer(k)).wait_recv()
            a_pass(chunk, z_peer(k), partner).start()
            return carry

        lax.fori_loop(1, ZS, step, 0)
        ax_copy(chunk, z_me).wait_recv()
        first, count = CHUNKS[chunk]
        got_a[partner, pl.ds(first, count)] = stage_a[z_me, pl.ds(first, count)]

    def a_wait(chunk):
        def step(k, carry):
            a_copy(chunk, z_me, x_me * ZS + z_peer(k)).wait_recv()
            a_pass(chunk, z_me, (1 - x_me) * ZS + z_peer(k)).wait_recv()
            return carry

        lax.fori_loop(1, ZS, step, 0)

    def a_done(chunk):
        def step(k, carry):
            a_copy(chunk, z_peer(k), e).wait_send()
            a_pass(chunk, z_peer(k), partner).wait_send()
            return carry

        def step_x(z, carry):
            ax_copy(chunk, z).wait_send()
            return carry

        lax.fori_loop(1, ZS, step, 0)
        lax.fori_loop(0, ZS, step_x, 0)

    pl.semaphore_wait(barrier, ENS - 1 + XS * (LATS - 1))
    for chunk in range(len(CHUNKS)):
        a_start(chunk)
    for index in range(EARLY, LOADS):
        retile_part(index)
    ax_start(0)

    def table_rows(index, carry):
        rows = pl.ds(pl.multiple_of(index * 64, 64), 64)
        lane = lax.broadcasted_iota(jnp.int32, (64, 128), 1).astype(F32)
        row = lax.broadcasted_iota(jnp.int32, (64, 128), 0)
        group = wave_rows[pl.ds(index // 4, 1), :].astype(F32)
        at = lax.rem(index, 4) * 32 + row // 2
        wave = jnp.sum(
            jnp.where(lax.broadcasted_iota(jnp.int32, (64, 128), 1) == at, group, 0.0),
            axis=1,
            keepdims=True,
        )

        def angles(turns):
            turns = turns - LON * jnp.floor(turns * (1.0 / LON))
            return turns * (2.0 * math.pi / LON)

        fine = angles(wave * lane)
        coarse = angles(wave * (128.0 * jnp.minimum(lane, 15.0)))
        cos_b, sin_b = jnp.cos(fine), jnp.sin(fine)
        factor = 1.0 / math.sqrt(LON)
        cos_a, sin_a = jnp.cos(coarse) * factor, jnp.sin(coarse) * factor
        real = lax.rem(row, 2) == 0
        first = jnp.where(real, cos_a, -sin_a)
        second = jnp.where(real, -sin_a, -cos_a)
        for lane_block in range(FULL + 1):
            width = min(128, LON - lane_block * 128)
            value = first[:, lane_block : lane_block + 1] * cos_b
            value = value + second[:, lane_block : lane_block + 1] * sin_b
            table[rows, pl.ds(lane_block * 128, width)] = value[:, :width].astype(BF16)
        return carry

    lax.fori_loop(0, COLS // 64, table_rows, 0)

    def forward(index, carry):
        lanes = pl.ds(pl.multiple_of(index * 384, 384), 384)
        value = lax.dot_general(
            table[...], mem[lanes, :], (((1,), (1,)), ((), ())), preferred_element_type=F32
        )
        send[:, lanes] = value.astype(BF16)
        return carry

    lax.fori_loop(0, ROWS // 384, forward, 0)

    per_plane = COLS // PLANE
    per_z = COLS // ZS

    def plane_copy(source, got, s_sem, r_sem, peer, slot):
        return pltpu.make_async_remote_copy(
            src_ref=source.at[pl.ds(peer * per_plane, per_plane)],
            dst_ref=got.at[pl.ds(slot * per_plane, per_plane)],
            send_sem=s_sem.at[peer],
            recv_sem=r_sem.at[slot],
            device_id={"ens": lax.rem(peer, XS) * ZS + z_me, "lat": peer // XS},
            device_id_type=MESH,
        )

    def z_copy(source, got, s_sem, r_sem, peer, slot):
        return pltpu.make_async_remote_copy(
            src_ref=source.at[pl.ds(peer * per_z, per_z)],
            dst_ref=got.at[pl.ds(slot * per_z, per_z)],
            send_sem=s_sem.at[peer],
            recv_sem=r_sem.at[slot],
            device_id={"ens": x_me * ZS + peer},
            device_id_type=MESH,
        )

    def exchange(copy, count, peer_of, me, size, got, s_sem, r_sem):
        def start(k, carry):
            copy(send, got, s_sem, r_sem, peer_of(k), me).start()
            return carry

        lax.fori_loop(1, count, start, 0)
        mine = pl.ds(pl.multiple_of(me * size, size), size)
        got[mine, :] = send[mine, :]

    def finish_near(copy, count, peer_of, me, got, s_sem, r_sem):
        for k in (1, 2, 3, 4):
            copy(send, got, s_sem, r_sem, me, peer_of(k)).wait_recv()

    def finish_far(copy, count, peer_of, me, got, s_sem, r_sem):
        for k in range(5, count):
            copy(send, got, s_sem, r_sem, me, peer_of(k)).wait_recv()
        for k in range(1, count):
            copy(send, got, s_sem, r_sem, peer_of(k), me).wait_send()

    def finish(copy, count, peer_of, me, got, s_sem, r_sem):
        def wait(k, carry):
            copy(send, got, s_sem, r_sem, peer_of(k), me).wait_send()
            copy(send, got, s_sem, r_sem, me, peer_of(k)).wait_recv()
            return carry

        lax.fori_loop(1, count, wait, 0)

    def widen(got):
        def step(index, carry):
            rows = pl.ds(pl.multiple_of(index * 48, 48), 48)
            for pair in range(PAIRS):
                wide[pair, rows, :] = got[rows, pl.ds(pair * 128, 128)].astype(F32)
            return carry

        lax.fori_loop(0, COLS // 48, step, 0)

    exchange(plane_copy, PLANE, plane_peer, g_me, per_plane, got_b1, b1_send, b1_recv)

    tgt_load.wait()

    def target_tile(index, carry):
        tile = e * OWN + index
        field = tile // FIELD_TILES
        place = tile - field * FIELD_TILES

        @pl.when(jnp.logical_and(place < FIELD_TILES - 1, tile < TILES))
        def _():
            block = place // FULL
            lane = place - block * FULL
            rows = pl.multiple_of(field * BAND + block * 16, 16)
            own_target[index] = tgt[
                pl.ds(rows, 16), pl.ds(pl.multiple_of(lane * 128, 128), 128)
            ].astype(F32)

        @pl.when(jnp.logical_and(place == FIELD_TILES - 1, tile < TILES))
        def _():
            rows = pl.multiple_of(field * BAND, BAND)
            tails = [
                tgt[pl.ds(rows + 16 * block, 16), pl.ds(FULL * 128, TAIL)].astype(F32)
                for block in range(BLOCKS)
            ]
            own_target[index] = jnp.concatenate(tails, axis=1)

        @pl.when(tile >= TILES)
        def _():
            own_target[index] = jnp.zeros((16, 128), F32)

        return carry

    lax.fori_loop(0, OWN, target_tile, 0)
    field_first = (e * OWN) // FIELD_TILES
    scores[...] = jnp.zeros_like(scores)
    for b in range(BATCHES):
        for v in range(FIELDS // BATCHES):
            for s in range(DEV_SLOTS):
                row = (b * (FIELDS // BATCHES) + v) * PARTS + 2 * s
                tspec[pl.ds(row, 2), :] = tsp[b, v, s].astype(F32)
    tspec[pl.ds(ENTRIES, GROUPS * 8 - ENTRIES), :] = jnp.zeros((GROUPS * 8 - ENTRIES, DEGREES), F32)
    spec_sum[...] = jnp.zeros_like(spec_sum)

    a_forward(0)
    finish(plane_copy, PLANE, plane_peer, g_me, got_b1, b1_send, b1_recv)
    widen(got_b1)

    def regroup_b(peer, carry):
        for pair in range(PAIRS):
            for piece in range(PARTS):
                value = wide[pair, pl.ds(peer * PARTS + piece, PLANE, stride=per_plane), :]
                rows = pl.multiple_of(peer * per_z + PLANE * piece, PLANE)
                send[pl.ds(rows, PLANE), pl.ds(pair * 128, 128)] = value.astype(BF16)
        return carry

    lax.fori_loop(0, ZS, regroup_b, 0)
    exchange(z_copy, ZS, z_peer, z_me, per_z, got_b2, b2_send, b2_recv)
    ax_start(1)
    ax_start(2)

    def grid_tile(index, carry):
        def load(member, inner):
            xs[member] = got_a[member, index].astype(F32)
            return inner

        lax.fori_loop(0, ENS, load, 0, unroll=True)
        for top in (0, 8):
            rows = pl.ds(top, 8)
            score, slope = crps_block(xs[:, rows, :], own_target[index, rows, :])
            ys[:, rows, :] = slope
            part[rows, :] = score

        def store(member, inner):
            got_a[member, index] = ys[member].astype(BF16)
            return inner

        lax.fori_loop(0, ENS, store, 0, unroll=True)
        tile = e * OWN + index
        field = tile // FIELD_TILES
        place = tile - field * FIELD_TILES
        local = field - field_first

        @pl.when(place < FIELD_TILES - 1)
        def _():
            rows = pl.ds(pl.multiple_of(place // FULL * 16, 16), 16)
            scores[local, rows, :] = scores[local, rows, :] + part[...]

        @pl.when(place == FIELD_TILES - 1)
        def _():
            segment = lax.broadcasted_iota(jnp.int32, (16, 128), 1) // TAIL
            for block in range(BLOCKS):
                rows = pl.ds(16 * block, 16)
                scores[local, rows, :] = scores[local, rows, :] + jnp.where(
                    segment == block, part[...], 0.0
                )

        return carry

    def dx_copy(chunk, z):
        first, count = CHUNKS[chunk]
        return pltpu.make_async_remote_copy(
            src_ref=got_a.at[(1 - x_me) * ZS + z, pl.ds(first, count)],
            dst_ref=stage_d.at[z, pl.ds(first, count)],
            send_sem=dx_send.at[chunk, z],
            recv_sem=dx_recv.at[chunk, z],
            device_id={"ens": partner},
            device_id_type=MESH,
        )

    def d_copy(chunk, z, slot):
        first, count = CHUNKS[chunk]
        return pltpu.make_async_remote_copy(
            src_ref=got_a.at[x_me * ZS + z, pl.ds(first, count)],
            dst_ref=got_d.at[pl.ds(slot * OWN + first, count)],
            send_sem=d_send.at[chunk, z],
            recv_sem=d_recv.at[chunk, slot],
            device_id={"ens": x_me * ZS + z},
            device_id_type=MESH,
        )

    def d_pass(chunk, z, slot):
        first, count = CHUNKS[chunk]
        return pltpu.make_async_remote_copy(
            src_ref=stage_d.at[z, pl.ds(first, count)],
            dst_ref=got_d.at[pl.ds(slot * OWN + first, count)],
            send_sem=d_send.at[chunk, ZS + z],
            recv_sem=d_recv.at[chunk, slot],
            device_id={"ens": x_me * ZS + z},
            device_id_type=MESH,
        )

    def d_keep(chunk):
        first, count = CHUNKS[chunk]
        return pltpu.make_async_copy(
            got_a.at[e, pl.ds(first, count)],
            got_d.at[pl.ds(e * OWN + first, count)],
            keep_sem.at[chunk, 0],
        )

    def d_cross(chunk):
        first, count = CHUNKS[chunk]
        return pltpu.make_async_copy(
            stage_d.at[z_me, pl.ds(first, count)],
            got_d.at[pl.ds(partner * OWN + first, count)],
            keep_sem.at[chunk, 1],
        )

    def dx_start(chunk):
        def step(k, carry):
            dx_copy(chunk, z_peer(k)).start()
            return carry

        lax.fori_loop(1, ZS + 1, step, 0)

    def d_start(chunk):
        def step(k, carry):
            d_copy(chunk, z_peer(k), e).start()
            return carry

        lax.fori_loop(1, ZS, step, 0)
        d_keep(chunk).start()

    def d_forward(chunk):
        def step(k, carry):
            dx_copy(chunk, z_peer(k)).wait_recv()
            d_pass(chunk, z_peer(k), partner).start()
            return carry

        lax.fori_loop(1, ZS, step, 0)
        dx_copy(chunk, z_me).wait_recv()
        d_cross(chunk).start()

    def d_wait(chunk):
        def step_send(k, carry):
            d_copy(chunk, z_peer(k), e).wait_send()
            d_pass(chunk, z_peer(k), partner).wait_send()
            return carry

        def step(k, carry):
            d_copy(chunk, z_me, x_me * ZS + z_peer(k)).wait_recv()
            d_pass(chunk, z_me, (1 - x_me) * ZS + z_peer(k)).wait_recv()
            return carry

        def step_x(z, carry):
            dx_copy(chunk, z).wait_send()
            return carry

        lax.fori_loop(0, ZS, step_x, 0)
        d_keep(chunk).wait()
        d_cross(chunk).wait()
        lax.fori_loop(1, ZS, step_send, 0)
        lax.fori_loop(1, ZS, step, 0)

    def grid_chunk(chunk):
        a_wait(chunk)
        first, count = CHUNKS[chunk]
        lax.fori_loop(first, first + count, grid_tile, 0)

    grid_chunk(0)
    dx_start(0)

    finish_near(z_copy, ZS, z_peer, z_me, got_b2, b2_send, b2_recv)
    a_forward(1)
    finish_far(z_copy, ZS, z_peer, z_me, got_b2, b2_send, b2_recv)
    a_forward(2)
    widen(got_b2)
    low = lax.broadcasted_iota(jnp.int32, (16, 128), 1) < 64

    def swap(even, odd):
        first = jnp.where(low, even, pltpu.roll(odd, 64, 1))
        second = jnp.where(low, pltpu.roll(even, 64, 1), odd)
        return first, second

    half_rows = 2 * PAIRS * ENS

    def legendre_in(index, carry):
        pair = index // PARTS
        piece = index - pair * PARTS
        slot = piece // 2
        c = piece - 2 * slot
        row = pl.multiple_of((c * PAIRS + pair) * ENS, ENS)
        for twin in range(LATS // 2):
            start = piece * PLANE + 2 * XS * twin
            rows = [wide[pair, pl.ds(start + i, ZS, stride=per_z), :] for i in range(2 * XS)]
            even = jnp.concatenate(rows[:XS], axis=0)
            odd = jnp.concatenate(rows[XS:], axis=0)
            first, second = swap(even, odd)
            mixed[slot, pl.ds(row, ENS), pl.ds(twin * 128, 128)] = first.astype(BF16)
            mixed[slot, pl.ds(row + half_rows, ENS), pl.ds(twin * 128, 128)] = second.astype(BF16)
        return carry

    lax.fori_loop(0, PAIRS * PARTS, legendre_in, 0)
    for lane_block in range(DEGREES // 128):
        spectral[lane_block, pl.ds(ENTRIES * ENS, GROUPS * 8 * ENS - ENTRIES * ENS), :] = jnp.zeros(
            (GROUPS * 8 * ENS - ENTRIES * ENS, 128), F32
        )

    leg_load.wait()

    def analysis(slot, carry):
        value = jnp.dot(mixed[slot], leg[slot], preferred_element_type=F32)
        for field in range(FIELDS):
            for c in range(2):
                row = (field % 2) * half_rows + (c * PAIRS + field // 2) * ENS
                to = pl.multiple_of((field * PARTS + 2 * slot + c) * ENS, ENS)
                for lane_block in range(DEGREES // 128):
                    spectral[lane_block, pl.ds(to, ENS), :] = value[
                        row : row + ENS, lane_block * 128 : lane_block * 128 + 128
                    ]
        return carry

    lax.fori_loop(0, DEV_SLOTS, analysis, 0)

    first_slot = (q_me * ENS + e) * DEV_SLOTS
    slot_waves = [wnum[first_slot + s] for s in range(DEV_SLOTS)]

    def spectral_group(index, carry):
        group = index // (DEGREES // 128)
        lane_block = index - group * (DEGREES // 128)
        entry = group * 8 + lax.broadcasted_iota(jnp.int32, (8, 128), 0)
        slot = lax.rem(entry // 2, DEV_SLOTS)
        wave = jnp.where(slot == 0, slot_waves[0], jnp.where(slot == 1, slot_waves[1], slot_waves[2]))
        degree = lane_block * 128 + lax.broadcasted_iota(jnp.int32, (8, 128), 1)
        usable = jnp.logical_and(degree >= wave, degree <= LMAX)
        weight = jnp.where(usable, jnp.where(wave == 0, 1.0, 2.0), 0.0)
        base = group * (8 * ENS)
        x = jnp.stack(
            [spectral[lane_block, pl.ds(base + m, 8, stride=ENS), :] for m in range(ENS)], axis=0
        )
        x = jnp.where(usable[None], x, 0.0).astype(BF16).astype(F32)
        rows = pl.ds(pl.multiple_of(group * 8, 8), 8)
        y = tspec[rows, pl.ds(pl.multiple_of(lane_block * 128, 128), 128)]
        score, slope = crps_block(x, y)
        spec_sum[rows, :] = spec_sum[rows, :] + score * weight
        slope = slope * weight[None]
        for m in range(ENS):
            spectral[lane_block, pl.ds(base + m, 8, stride=ENS), :] = slope[m]
        return carry

    lax.fori_loop(0, GROUPS * (DEGREES // 128), spectral_group, 0)

    def synthesis(slot, carry):
        for field in range(FIELDS):
            for c in range(2):
                row = (field % 2) * half_rows + (c * PAIRS + field // 2) * ENS
                at = pl.multiple_of((field * PARTS + 2 * slot + c) * ENS, ENS)
                for lane_block in range(DEGREES // 128):
                    mixed[slot, pl.ds(row, ENS), pl.ds(lane_block * 128, 128)] = spectral[
                        lane_block, pl.ds(at, ENS), :
                    ].astype(BF16)
        value = lax.dot_general(
            mixed[slot, :, pl.ds(0, DEGREES)], leg[slot], (((1,), (1,)), ((), ())),
            preferred_element_type=F32,
        )
        for pair in range(PAIRS):
            for c in range(2):
                row = (c * PAIRS + pair) * ENS
                for twin in range(LATS // 2):
                    lanes = slice(twin * 128, twin * 128 + 128)
                    even, odd = swap(
                        value[row : row + ENS, lanes],
                        value[row + half_rows : row + half_rows + ENS, lanes],
                    )
                    start = (2 * slot + c) * PLANE + 2 * XS * twin
                    for i in range(XS):
                        members = slice(i * ZS, i * ZS + ZS)
                        wide[pair, pl.ds(start + i, ZS, stride=per_z), :] = even[members]
                        wide[pair, pl.ds(start + XS + i, ZS, stride=per_z), :] = odd[members]
        return carry

    lax.fori_loop(0, DEV_SLOTS, synthesis, 0)

    def narrow(index, carry):
        rows = pl.ds(pl.multiple_of(index * 48, 48), 48)
        for pair in range(PAIRS):
            send[rows, pl.ds(pair * 128, 128)] = wide[pair, rows, :].astype(BF16)
        return carry

    lax.fori_loop(0, COLS // 48, narrow, 0)
    exchange(z_copy, ZS, z_peer, z_me, per_z, got_c1, c1_send, c1_recv)
    grid_chunk(1)
    dx_start(1)
    grid_chunk(2)
    dx_start(2)
    finish_near(z_copy, ZS, z_peer, z_me, got_c1, c1_send, c1_recv)
    d_start(0)
    d_forward(0)

    lane = lax.broadcasted_iota(jnp.int32, (BAND, 128), 1)
    total = jnp.zeros((BAND, 128), F32)
    for local in range(3):
        rows_sum = jnp.sum(scores[local], axis=1, keepdims=True) * (1.0 / LON)
        total = total + jnp.where(lane == field_first + local, rows_sum, 0.0)
    turn = lax.rem(lax.broadcasted_iota(jnp.int32, (BAND, 128), 0), 4)
    packed = total
    for place in range(1, 4):
        packed = jnp.where(turn == place, pltpu.roll(total, 32 * place, 1), packed)
    for peer in range(ENS):
        score_sum[peer] = jnp.sum(packed[4 * peer : 4 * peer + 4], axis=0, keepdims=True)

    def s_copy(peer, slot):
        return pltpu.make_async_remote_copy(
            src_ref=score_sum.at[peer],
            dst_ref=got_s.at[slot],
            send_sem=s_send.at[peer],
            recv_sem=s_recv.at[slot],
            device_id={"ens": peer},
            device_id_type=MESH,
        )

    def s_start(k, carry):
        s_copy(ens_peer(k), e).start()
        return carry

    lax.fori_loop(1, ENS, s_start, 0)
    got_s[e] = score_sum[e]

    finish_far(z_copy, ZS, z_peer, z_me, got_c1, c1_send, c1_recv)
    d_start(1)
    d_forward(1)
    d_start(2)
    d_forward(2)
    widen(got_c1)

    def regroup_c(place, carry):
        rows = pl.ds(pl.multiple_of(place * per_plane, per_plane), per_plane)
        for pair in range(PAIRS):
            send[rows, pl.ds(pair * 128, 128)] = wide[
                pair, pl.ds(place, per_plane, stride=PLANE), :
            ].astype(BF16)
        return carry

    lax.fori_loop(0, PLANE, regroup_c, 0)
    exchange(plane_copy, PLANE, plane_peer, g_me, per_plane, got_c2, c2_send, c2_recv)
    sums = jnp.sum(spec_sum[...], axis=1, keepdims=True) * (1.0 / (2.0 * (LMAX + 1)))
    entry = lax.broadcasted_iota(jnp.int32, (GROUPS * 8, 128), 0)
    variables = FIELDS // BATCHES
    place = lax.broadcasted_iota(jnp.int32, (GROUPS * 8, 128), 1)
    sums = jnp.where(place == lax.rem(entry // PARTS, variables), sums, 0.0)
    for b in range(BATCHES):
        for slot in range(DEV_SLOTS):
            chosen = jnp.logical_and(
                entry // (PARTS * variables) == b, lax.rem(entry, PARTS) // 2 == slot
            )
            small[pl.ds(8 + b * DEV_SLOTS + slot, 1), :] = jnp.sum(
                jnp.where(chosen, sums, 0.0), axis=0, keepdims=True
            )
    finish(plane_copy, PLANE, plane_peer, g_me, got_c2, c2_send, c2_recv)

    def backward(index, carry):
        lanes = pl.ds(pl.multiple_of(index * 384, 384), 384)
        grad[lanes, :] = lax.dot_general(
            got_c2[:, lanes], table[...], (((0,), (0,)), ((), ())), preferred_element_type=F32
        )
        return carry

    lax.fori_loop(0, ROWS // 384, backward, 0)

    def s_wait(k, carry):
        s_copy(ens_peer(k), e).wait_send()
        s_copy(e, ens_peer(k)).wait_recv()
        return carry

    for chunk in range(len(CHUNKS)):
        a_done(chunk)
    lax.fori_loop(1, ENS, s_wait, 0)
    small[pl.ds(0, 1), :] = jnp.sum(got_s[...], axis=0)
    for chunk in range(len(CHUNKS)):
        d_wait(chunk)


def combine_kernel(got_d, grad, small, out_hbm, row_out, spec_out, out, out_sem):
    variables = FIELDS // BATCHES
    for b in range(BATCHES):
        for row in range(4):
            lanes = pl.ds(32 * row + b * variables, variables)
            row_out[b, pl.ds(row, 1), :] = small[pl.ds(0, 1), lanes]
        spec_out[b] = small[pl.ds(8 + b * DEV_SLOTS, DEV_SLOTS), pl.ds(0, variables)]

    def combine(field, carry):
        top = pl.multiple_of(field * BAND, BAND)
        tail = got_d[field * FIELD_TILES + FIELD_TILES - 1].astype(F32)
        for block in range(BLOCKS):
            rows = pl.ds(top + 16 * block, 16)
            for lane_block in range(FULL):
                lanes = pl.ds(lane_block * 128, 128)
                slope = got_d[field * FIELD_TILES + block * FULL + lane_block].astype(F32)
                out[rows, lanes] = (grad[rows, lanes] + slope).astype(BF16)
            lanes = pl.ds(FULL * 128, TAIL)
            moved = tail if block == 0 else pltpu.roll(tail, 128 - block * TAIL, 1)
            out[rows, lanes] = (grad[rows, lanes] + moved[:, :TAIL]).astype(BF16)
        return carry

    stores = []
    for step in range(STEPS):
        lax.fori_loop(step * (FIELDS // STEPS), (step + 1) * (FIELDS // STEPS), combine, 0)
        rows = pl.ds(step * (ROWS // STEPS), ROWS // STEPS)
        stores.append(pltpu.make_async_copy(out.at[rows], out_hbm.at[rows], out_sem.at[step]))
        stores[-1].start()
    for store in stores:
        store.wait()


def body(members, target, target_spectrum, legendre, wavenum):
    chunks = len(CHUNKS)
    vmem = pl.BlockSpec(memory_space=pltpu.VMEM)
    hbm = pl.BlockSpec(memory_space=pl.ANY)
    dma = pltpu.SemaphoreType.DMA
    slopes, grad, small = pl.pallas_call(
        body_kernel,
        out_shape=(
            pltpu.VMEM((ENS * OWN, 16, 128), BF16),
            pltpu.VMEM((ROWS, LON), F32),
            pltpu.VMEM((24, 128), F32),
        ),
        in_specs=[hbm, hbm, vmem, hbm, vmem, pl.BlockSpec(memory_space=pltpu.SMEM)],
        out_specs=(vmem, vmem, vmem),
        scratch_shapes=[
            pltpu.VMEM((ROWS, LON), BF16),
            pltpu.VMEM((ROWS, LON), BF16),
            pltpu.VMEM((DEV_SLOTS, LATITUDES, DEGREES), BF16),
            pltpu.VMEM((ENS * OWN, 16, 128), BF16),
            pltpu.VMEM((OWN, 16, 128), F32),
            pltpu.VMEM((ENS, OWN, 16, 128), BF16),
            pltpu.VMEM((ZS, OWN, 16, 128), BF16),
            pltpu.VMEM((ZS, OWN, 16, 128), BF16),
            pltpu.VMEM((COLS, LON), BF16),
            pltpu.VMEM((COLS, ROWS), BF16),
            pltpu.VMEM((COLS, ROWS), BF16),
            pltpu.VMEM((COLS, ROWS), BF16),
            pltpu.VMEM((COLS, ROWS), BF16),
            pltpu.VMEM((COLS, ROWS), BF16),
            pltpu.VMEM((PAIRS, COLS, 128), F32),
            pltpu.VMEM((DEV_SLOTS, FIELDS * 2 * ENS, LATITUDES), BF16),
            pltpu.VMEM((DEGREES // 128, GROUPS * 8 * ENS, 128), F32),
            pltpu.VMEM((GROUPS * 8, DEGREES), F32),
            pltpu.VMEM((GROUPS * 8, 128), F32),
            pltpu.VMEM((16, 128), F32),
            pltpu.VMEM((ENS, 16, 128), F32),
            pltpu.VMEM((ENS, 16, 128), F32),
            pltpu.VMEM((3, BAND, 128), F32),
            pltpu.VMEM((ENS, 1, 128), F32),
            pltpu.VMEM((ENS, 1, 128), F32),
            dma((chunks, ZS)), dma((chunks, ZS)),
            dma((chunks, ZS)), dma((chunks, ZS)),
            dma((chunks, ENS)), dma((chunks, ENS)),
            dma((chunks, ENS)), dma((chunks, ENS)),
            dma((PLANE,)), dma((PLANE,)),
            dma((ZS,)), dma((ZS,)),
            dma((ZS,)), dma((ZS,)),
            dma((PLANE,)), dma((PLANE,)),
            dma((ENS,)), dma((ENS,)),
            dma((LOADS,)), dma, dma, dma((chunks, 2)),
        ],
        compiler_params=pltpu.CompilerParams(
            collective_id=0, has_side_effects=True, vmem_limit_bytes=48 * 2**20
        ),
    )(
        members.reshape(ROWS, LON),
        target.reshape(ROWS, LON),
        target_spectrum,
        legendre,
        wavenum.reshape(SLOTS // 128, 128),
        wavenum,
    )
    variables = FIELDS // BATCHES
    member_grad, row_score, spec_score = pl.pallas_call(
        combine_kernel,
        out_shape=(
            jax.ShapeDtypeStruct((ROWS, LON), BF16),
            jax.ShapeDtypeStruct((BATCHES, 4, variables), F32),
            jax.ShapeDtypeStruct((BATCHES, DEV_SLOTS, variables), F32),
        ),
        in_specs=[vmem, vmem, vmem],
        out_specs=(hbm, vmem, vmem),
        scratch_shapes=[pltpu.VMEM((ROWS, LON), BF16), dma((STEPS,))],
        compiler_params=pltpu.CompilerParams(vmem_limit_bytes=16 * 2**20),
    )(slopes, grad, small)
    return (
        member_grad.reshape(members.shape),
        row_score.transpose(0, 2, 1),
        spec_score.transpose(0, 2, 1),
    )


def solution(mesh):
    in_specs = (
        P("ens", None, "var", "lat", None),
        P(None, "var", "lat", None),
        P(None, "var", ("lat", "ens"), None, None),
        P(("lat", "ens"), None, None),
        P(),
    )
    out_specs = (
        P("ens", None, "var", "lat", None),
        P(None, "var", ("lat", "ens")),
        P(None, "var", ("lat", "ens")),
    )
    return jax.shard_map(body, mesh=mesh, in_specs=in_specs, out_specs=out_specs, check_vma=False)
```
